32 devices in a mesh: ctx: 8 (over z, x), fsdp: 4 (over y, core).
Axes of the slice: x: 2, y: 2, z: 4, core: 2. Of those that a mesh axis runs over, the one named last changes fastest.
Arguments:
- tokens: bfloat16 [4096, 640], P(('ctx', 'fsdp')), may hold values from -6 to 6
- cotangent: bfloat16 [4096, 640], P(('ctx', 'fsdp')), may hold values from -6 to 6
- block_order: int32 [16], replicated, may hold values from 0 to 15, as said below
- query_weight: bfloat16 [640, 1024], P('fsdp'), may hold values from -0.25 to 0.25
- key_weight: bfloat16 [640, 256], P('fsdp'), may hold values from -0.25 to 0.25
- value_weight: bfloat16 [640, 256], P('fsdp'), may hold values from -0.25 to 0.25
- out_weight: bfloat16 [1024, 640], P('fsdp'), may hold values from -0.1875 to 0.1875
- gate_weight: bfloat16 [640, 2048], P(None, 'fsdp'), may hold values from -0.25 to 0.25
- up_weight: bfloat16 [640, 2048], P(None, 'fsdp'), may hold values from -0.25 to 0.25
- down_weight: bfloat16 [2048, 640], P('fsdp'), may hold values from -0.125 to 0.125
- norm_gains: bfloat16 [4, 640], P(None, 'fsdp'), may hold values from 0.5 to 1.5
- head_gains: bfloat16 [2, 256], P(None, 'fsdp'), may hold values from 0.5 to 1.5
Outputs:
- output: bfloat16 [4096, 640], P(('ctx', 'fsdp'))
- input_grad: float32 [4096, 640], P(('ctx', 'fsdp'))
- grad_query_weight: float32 [640, 1024], P('fsdp')
- grad_key_weight: float32 [640, 256], P('fsdp')
- grad_value_weight: float32 [640, 256], P('fsdp')
- grad_out_weight: float32 [1024, 640], P('fsdp')
- grad_gate_weight: float32 [640, 2048], P(None, 'fsdp')
- grad_up_weight: float32 [640, 2048], P(None, 'fsdp')
- grad_down_weight: float32 [2048, 640], P('fsdp')
- grad_norm_gains: float32 [4, 640], P(None, 'fsdp')
- grad_head_gains: float32 [2, 256], P(None, 'fsdp')
The draws below stay inside these ranges and needn't reach their ends.
Inputs may be any that keep to these rules, and one draw needn't show every extreme that they name: block_order is a permutation in which entries 2c and 2c + 1 sum to 15 for every c.
All inputs are finite; a program needn't handle non-finite values.
Results may differ from the reference program's by a relative error of at most 0.019.
Values may be sent and summed in bfloat16 or wider, within the bound.
No kernel may reach another device: no remote copies, remote signals or barrier semaphores. Data moves between devices by JAX's collectives and lax.ppermute only.
A program may use at most 128 MiB of HBM per device.

```python
import math
import jax
import jax.numpy as jnp
from jax import lax

D = 640
HEADS = 4
HEAD_DIM = 256
FF = 2048
TOK_DEV = 128
BLOCK = 64
BLOCKS = 16
SEQ_LEN = 1024
SEQS = 4
TOKENS = 4096
N_CTX = 8


def draw_block_order(key, part):
    key = jax.random.fold_in(key, 7)
    pairs = jax.random.permutation(key, BLOCKS // 2).astype(jnp.int32)
    mirror = (BLOCKS - 1 - pairs).astype(jnp.int32)
    return jnp.stack([pairs, mirror], axis=1).reshape(BLOCKS).astype(jnp.int32)


def block_scale(key, shape, shards, least, largest):
    gain = 1.0
    for axis_at, shards_of in shards:
        draws = jax.random.uniform(jax.random.fold_in(jax.random.fold_in(key, 6), axis_at), (shards_of,), jnp.float32, least / len(shards), largest / len(shards))
        gain = gain * jnp.repeat(jnp.exp(draws), shape[axis_at] // shards_of).reshape((-1,) + (1,) * (len(shape) - 1 - axis_at))
    return gain


def bell_draw(own_key, dims, width, reach, pieces=(), held_as=jnp.bfloat16):
    values = jax.random.normal(own_key, dims, jnp.float32) * width
    if len(pieces) > 0:
        values = block_scale(own_key, dims, pieces, -0.22, 0.18) * values
    return jnp.clip(values, min=-reach, max=reach).astype(held_as)


def setup_inputs(seed: int = 0) -> dict:
    splits = jax.random.split(jax.random.key(seed), 13)
    return {
        "tokens": bell_draw(splits[0], (TOKENS, D), 1.0, 6.0, ((0, 32),)),
        "cotangent": bell_draw(splits[1], (TOKENS, D), 1.0, 6.0, ((0, 32),)),
        "block_order": draw_block_order(jax.random.fold_in(splits[12], 71), 0),
        "query_weight": bell_draw(splits[3], (D, HEADS * HEAD_DIM), D ** -0.5, 0.25, ((0, 4),)),
        "key_weight": bell_draw(splits[4], (D, HEAD_DIM), D ** -0.5, 0.25, ((0, 4),)),
        "value_weight": bell_draw(splits[5], (D, HEAD_DIM), D ** -0.5, 0.25, ((0, 4),)),
        "out_weight": bell_draw(splits[6], (HEADS * HEAD_DIM, D), (HEADS * HEAD_DIM) ** -0.5, 0.1875, ((0, 4),)),
        "gate_weight": bell_draw(splits[7], (D, FF), D ** -0.5, 0.25, ((1, 4),)),
        "up_weight": bell_draw(splits[8], (D, FF), D ** -0.5, 0.25, ((1, 4),)),
        "down_weight": bell_draw(splits[9], (FF, D), FF ** -0.5, 0.125, ((0, 4),)),
        "norm_gains": jnp.clip(1.0 + 0.1 * jax.random.normal(splits[10], (4, D), jnp.float32), 0.5, 1.5).astype(jnp.bfloat16),
        "head_gains": jnp.clip(1.0 + 0.1 * jax.random.normal(splits[11], (2, HEAD_DIM), jnp.float32), 0.5, 1.5).astype(jnp.bfloat16),
    }


@jax.custom_vjp
def low(v):
    return lax.optimization_barrier(v.astype(jnp.bfloat16)).astype(jnp.float32)

@jax.custom_vjp
def low_back(v):
    return v

def low_keep(v):
    return (low(v), None)

def low_pass(kept, grad):
    return (grad,)

def back_keep(v):
    return (v, None)

def back_low(kept, grad):
    return (low(grad),)
low.defvjp(low_keep, low_pass)
low_back.defvjp(back_keep, back_low)
NORM_EPS = 1e-06
ROPE_BASE = 1000000.0
HIGHEST_PRECISION = lax.Precision.HIGHEST

def norm_scale(values, scales):
    return values * lax.rsqrt(lax.optimization_barrier(jnp.mean(values * values, axis=-1, keepdims=True)) + NORM_EPS) * scales

def rotate(values, cosine, sine_table):
    half_size = values.shape[-1] // 2
    first_half = values[..., :half_size]
    second_half = values[..., half_size:]
    return jnp.concatenate([first_half * cosine - second_half * sine_table, second_half * cosine + first_half * sine_table], axis=-1)

def rope_tables(positions):
    freq_index = jnp.arange(HEAD_DIM // 2, dtype=jnp.float32)
    inv_freq = ROPE_BASE ** (-2.0 * freq_index / HEAD_DIM)
    angles = positions.astype(jnp.float32)[:, None] * inv_freq[None, :]
    return (jnp.cos(angles), jnp.sin(angles))

def matmul(left, right):
    return jnp.dot(left, right, precision=HIGHEST_PRECISION, preferred_element_type=jnp.float32)

def sequence_layer(weights, source, cosine, sine_table, positions, score_bound):
    query_weight, key_weight, value_weight, out_weight, gate_weight, up_weight, down_weight, norm_gains, head_gains = weights
    score_scale = 1.0 / math.sqrt(HEAD_DIM)
    block_len = min(256, SEQ_LEN)
    normed_low = low(norm_scale(source, norm_gains[0]))
    query_raw = low_back(matmul(normed_low, query_weight))
    key_raw = low_back(matmul(normed_low, key_weight))
    value_low = low(low_back(matmul(normed_low, value_weight)))
    query_norm = norm_scale(query_raw.reshape(SEQ_LEN, HEADS, HEAD_DIM), head_gains[0])
    query_rot = low(rotate(query_norm, cosine[:, None, :], sine_table[:, None, :]))
    key_rot = low(rotate(norm_scale(key_raw, head_gains[1]), cosine, sine_table))
    query_blocks = query_rot.reshape(SEQ_LEN // block_len, block_len, HEADS, HEAD_DIM)
    position_blocks = positions.reshape(SEQ_LEN // block_len, block_len)

    def attend(item_pair):
        query_part, part_positions = item_pair
        raw_score = low_back(jnp.einsum('qhd,kd->hqk', query_part, key_rot, precision=HIGHEST_PRECISION))
        allowed = positions[None, None, :] <= part_positions[None, :, None]
        exp_terms = jnp.where(allowed, jnp.exp(raw_score * score_scale - score_bound), 0.0)
        row_total = lax.optimization_barrier(jnp.sum(exp_terms, axis=-1))
        numerator = low_back(jnp.einsum('hqk,kd->hqd', low(exp_terms), value_low, precision=HIGHEST_PRECISION))
        return jnp.transpose(numerator / row_total[..., None], (1, 0, 2)).reshape(block_len, HEADS * HEAD_DIM)
    attended = lax.map(jax.checkpoint(attend), (query_blocks, position_blocks))
    attended_low = low(attended.reshape(SEQ_LEN, HEADS * HEAD_DIM))
    branch = low_back(matmul(attended_low, out_weight))
    middle = source + norm_scale(branch, norm_gains[1])
    ff_in = low(norm_scale(middle, norm_gains[2]))
    gate_out = low_back(matmul(ff_in, gate_weight))
    up_out = low_back(matmul(ff_in, up_weight))
    hidden = low(jax.nn.gelu(gate_out, approximate=True) * up_out)
    mixed_out = low_back(matmul(hidden, down_weight))
    return middle + norm_scale(mixed_out, norm_gains[3])

def to_sequences(array):
    return array.astype(jnp.float32).reshape(N_CTX, SEQS, TOK_DEV, D).transpose(1, 0, 2, 3).reshape(SEQS, SEQ_LEN, D)

def from_sequences(array):
    return array.reshape(SEQS, N_CTX, TOK_DEV, D).transpose(1, 0, 2, 3).reshape(TOKENS, D)

def reference(tokens, cotangent, block_order, query_weight, key_weight, value_weight, out_weight, gate_weight, up_weight, down_weight, norm_gains, head_gains):
    weights = (query_weight.astype(jnp.float32), key_weight.astype(jnp.float32), value_weight.astype(jnp.float32), out_weight.astype(jnp.float32), gate_weight.astype(jnp.float32), up_weight.astype(jnp.float32), down_weight.astype(jnp.float32), norm_gains.astype(jnp.float32), head_gains.astype(jnp.float32))
    slot_rows = jnp.arange(SEQ_LEN, dtype=jnp.int32)
    positions = (block_order[slot_rows // BLOCK] * BLOCK + slot_rows % BLOCK).astype(jnp.int32)
    cosine, sine_table = rope_tables(positions)
    score_bound = math.sqrt(HEAD_DIM) * jnp.max(jnp.abs(weights[8][0])) * jnp.max(jnp.abs(weights[8][1]))
    inputs = to_sequences(tokens)
    incoming = to_sequences(cotangent)

    def forward(layer_weights, sequences):
        return lax.map(lambda source: sequence_layer(layer_weights, source, cosine, sine_table, positions, score_bound), sequences)
    result, pullback = jax.vjp(forward, weights, inputs)
    weight_grads, source_grads = pullback(incoming)
    return (from_sequences(result).astype(jnp.bfloat16), from_sequences(source_grads), weight_grads[0], weight_grads[1], weight_grads[2], weight_grads[3], weight_grads[4], weight_grads[5], weight_grads[6], weight_grads[7], weight_grads[8])
```

```python
import functools
import math

import jax
import jax.numpy as jnp
from jax import lax
from jax.experimental import pallas as pl
from jax.experimental.pallas import tpu as pltpu
from jax.sharding import PartitionSpec as P

HEADS = 4
HEAD_DIM = 256
NORM_EPS = 1e-06
ROPE_BASE = 1000000.0
BF = jnp.bfloat16
F32 = jnp.float32
MIB = 1024 * 1024


def dot(a, b):
    return lax.dot_general(a, b, (((1,), (0,)), ((), ())), preferred_element_type=F32)


def dot_nt(a, b):
    return lax.dot_general(a, b, (((1,), (1,)), ((), ())), preferred_element_type=F32)


def dot_tn(a, b):
    return lax.dot_general(a, b, (((0,), (0,)), ((), ())), preferred_element_type=F32)


def unit(v):
    r = lax.rsqrt(jnp.mean(v * v, axis=-1, keepdims=True) + NORM_EPS)
    return v * r, r


def norm_back(c, u, r, g):
    cg = c * g
    grad = r * (cg - u * jnp.mean(cg * u, axis=-1, keepdims=True))
    return grad, jnp.sum(c * u, axis=0, keepdims=True)


def rotate(v, cos, sin):
    half = v.shape[-1] // 2
    a, b = v[:, :half], v[:, half:]
    return jnp.concatenate([a * cos - b * sin, b * cos + a * sin], axis=-1)


def rotate_back(v, cos, sin):
    half = v.shape[-1] // 2
    a, b = v[:, :half], v[:, half:]
    return jnp.concatenate([a * cos + b * sin, b * cos - a * sin], axis=-1)


def assemble(f, blocks, scratch):
    rows = blocks[0].shape[0]
    for k, blk in enumerate(blocks):
        start = pl.multiple_of(jnp.bitwise_xor(f, k) * rows, 16)
        scratch[pl.ds(start, rows), :] = blk[...]


def call(kernel, outs, *args, scratch=(), vmem=40, flops=0, smem_first=False):
    specs = [pl.BlockSpec(memory_space=pltpu.VMEM)] * len(args)
    if smem_first:
        specs[0] = pl.BlockSpec(memory_space=pltpu.SMEM)
    moved = sum(math.prod(a.shape) * a.dtype.itemsize for a in args)
    return pl.pallas_call(
        kernel,
        out_shape=[jax.ShapeDtypeStruct(s, d) for s, d in outs],
        in_specs=specs,
        out_specs=[pl.BlockSpec(memory_space=pltpu.VMEM)] * len(outs),
        scratch_shapes=list(scratch),
        compiler_params=pltpu.CompilerParams(vmem_limit_bytes=vmem * MIB),
        cost_estimate=pl.CostEstimate(flops=flops, bytes_accessed=moved, transcendentals=0),
    )(*args)


def kv_kernel(nf, f_ref, tok, gains, hg, cos, sin, *rest):
    blocks, (normed_o, raw_o, kv_o, w) = rest[:nf], rest[nf:]
    assemble(f_ref[0], blocks, w)
    u, _ = unit(tok[...].astype(F32))
    normed = (u * gains[0:1, :]).astype(BF)
    normed_o[...] = normed
    out = dot(normed, w[...])
    key = out[:, :HEAD_DIM]
    raw_o[...] = key
    u, _ = unit(key)
    kv_o[:, :HEAD_DIM] = rotate(u * hg[1:2, :], cos[...], sin[...]).astype(BF)
    kv_o[:, HEAD_DIM:] = out[:, HEAD_DIM:].astype(BF)


def query_kernel(nf, f_ref, normed, hg, cos, sin, *rest):
    blocks, (raw_o, q_o, w) = rest[:nf], rest[nf:]
    assemble(f_ref[0], blocks, w)
    for h in range(HEADS):
        raw = dot(normed[...], w[:, h * HEAD_DIM : (h + 1) * HEAD_DIM])
        k = jnp.bitwise_xor(f_ref[0], h)
        raw_o[k] = raw
        u, _ = unit(raw)
        q_o[k] = rotate(u * hg[0:1, :], cos[...], sin[...]).astype(BF)


def bound_of(hg):
    peak = jnp.max(jnp.abs(hg[...]), axis=1, keepdims=True)
    return math.sqrt(HEAD_DIM) * peak[0:1, :] * peak[1:2, :]


def tile_loop(count, step):
    if count == 1:
        step(0)
    else:

        def body(t, carry):
            step(t)
            return carry

        lax.fori_loop(0, count, body, 0)


def attend_kernel(tile, q, kv, hg, qpos, kpos, att_o, low_o, tot_o):
    scale = 1.0 / math.sqrt(HEAD_DIM)
    bound = bound_of(hg)
    count = kv.shape[0] // tile
    for k in range(HEADS):

        def step(t, k=k):
            rows = pl.ds(pl.multiple_of(t * tile, tile), tile) if count > 1 else slice(None)
            raw = dot_nt(q[k], kv[rows, :HEAD_DIM])
            allowed = kpos[:, rows] <= qpos[...]
            terms = jnp.where(allowed, jnp.exp(raw * scale - bound), 0.0)
            total = jnp.sum(terms, axis=1, keepdims=True)
            num = dot(terms.astype(BF), kv[rows, HEAD_DIM:])
            if count == 1:
                tot_o[k], att_o[k] = total, num
            else:
                tot_o[k] += total
                att_o[k] += num

        if count > 1:
            tot_o[k] = jnp.zeros_like(tot_o[k])
            att_o[k] = jnp.zeros_like(att_o[k])
        tile_loop(count, step)
        att = att_o[k] / tot_o[k]
        att_o[k] = att
        low_o[k] = att.astype(BF)


def gelu_parts(v):
    inner = 0.7978845608028654 * (v + 0.044715 * v * v * v)
    t = jnp.tanh(inner)
    value = 0.5 * v * (1.0 + t)
    slope = 0.5 * (1.0 + t) + 0.5 * v * (1.0 - t * t) * 0.7978845608028654 * (
        1.0 + 3 * 0.044715 * v * v
    )
    return value, slope


def ff_kernel(nf, tok, cot, gains, att, *rest):
    wo, wg, wu, wd = (rest[i * nf : (i + 1) * nf] for i in range(4))
    rest = rest[4 * nf :]
    out_o, fg_o, gbl_o, resid_o, gg_o = rest[:5]
    ex_o = rest[5 : 5 + nf]
    gate_s, up_s = rest[5 + nf :]
    d = tok.shape[1]
    width = wg[0].shape[1]
    heads = att.shape[0] // nf
    branch = None
    for k in range(nf):
        term = dot(att[k], wo[k][...])
        branch = term if branch is None else branch + term
    x = tok[...].astype(F32)
    ub, rb = unit(branch)
    middle = x + ub * gains[1:2, :]
    um, rm = unit(middle)
    ff_in = (um * gains[2:3, :]).astype(BF)
    fg_o[:, :d] = ff_in
    mixed = None
    for k in range(nf):
        gate = dot(ff_in, wg[k][...])
        up = dot(ff_in, wu[k][...])
        gate_s[k] = gate
        up_s[k] = up
        value, _ = gelu_parts(gate)
        hidden = (value * up).astype(BF)
        ex_o[k][:, :width] = hidden
        term = dot(hidden, wd[k][...])
        mixed = term if mixed is None else mixed + term
    ux, rx = unit(mixed)
    out_o[...] = (middle + ux * gains[3:4, :]).astype(BF)
    c = cot[...].astype(F32)
    grad_mixed, gain3 = norm_back(c, ux, rx, gains[3:4, :])
    gml = grad_mixed.astype(BF)
    fg_o[:, d:] = gml
    gff = None
    for k in range(nf):
        gh = dot_nt(gml, wd[k][...])
        value, slope = gelu_parts(gate_s[k])
        gg = (gh * up_s[k] * slope).astype(BF)
        gu = (gh * value).astype(BF)
        ex_o[k][:, width : 2 * width] = gg
        ex_o[k][:, 2 * width :] = gu
        term = dot_nt(gg, wg[k][...]) + dot_nt(gu, wu[k][...])
        gff = term if gff is None else gff + term
    grad, gain2 = norm_back(gff, um, rm, gains[2:3, :])
    grad_middle = c + grad
    grad_branch, gain1 = norm_back(grad_middle, ub, rb, gains[1:2, :])
    resid_o[...] = grad_middle
    gbl_o[...] = grad_branch.astype(BF)
    gg_o[...] = jnp.concatenate([gain1, gain2, gain3], axis=0)


def attend_back_kernel(nf, tile, f_ref, gbl, att, tot, q, qraw, kv, hg, cos, sin, qpos, kpos, *rest):
    wo = rest[:nf]
    gq_o, gh_o, gkv_o, sg_s, tg_s, acc, s_s, e_s = rest[nf:]
    scale = 1.0 / math.sqrt(HEAD_DIM)
    rows_q = gbl.shape[0]
    bound = bound_of(hg)
    count = kv.shape[0] // tile
    for k in range(HEADS):
        ga = dot_nt(gbl[...], wo[k][...])
        inv = 1.0 / tot[k]
        sg_s[k * rows_q : (k + 1) * rows_q, :] = (ga * inv).astype(BF)
        tg_s[k] = -jnp.sum(ga * att[k], axis=1, keepdims=True) * inv

    def step(t):
        rows = pl.ds(pl.multiple_of(t * tile, tile), tile) if count > 1 else slice(None)
        allowed = kpos[:, rows] <= qpos[...]
        for k in range(HEADS):
            mine = slice(k * rows_q, (k + 1) * rows_q)
            raw = dot_nt(q[k], kv[rows, :HEAD_DIM])
            terms = jnp.where(allowed, jnp.exp(raw * scale - bound), 0.0)
            e_s[mine, :] = terms.astype(BF)
            gp = dot_nt(sg_s[mine, :], kv[rows, HEAD_DIM:])
            s = (terms * (gp + tg_s[k]) * scale).astype(BF)
            s_s[mine, :] = s
            part = dot(s, kv[rows, :HEAD_DIM])
            if count == 1:
                acc[k] = part
            else:
                acc[k] += part
        queries = q[...].reshape(HEADS * rows_q, HEAD_DIM)
        gkv_o[rows, :HEAD_DIM] = dot_tn(s_s[...], queries).astype(BF)
        gkv_o[rows, HEAD_DIM:] = dot_tn(e_s[...], sg_s[...]).astype(BF)

    if count > 1:
        acc[...] = jnp.zeros_like(acc)
    tile_loop(count, step)
    gain = None
    for k in range(HEADS):
        u, r = unit(qraw[k])
        c = rotate_back(acc[k], cos[...], sin[...])
        grad, g = norm_back(c, u, r, hg[0:1, :])
        gain = g if gain is None else gain + g
        h = jnp.bitwise_xor(f_ref[0], k)
        gq_o[:, pl.ds(pl.multiple_of(h * HEAD_DIM, HEAD_DIM), HEAD_DIM)] = grad.astype(BF)
    gh_o[...] = gain


def input_back_kernel(nf, f_ref, tok, gkv, kraw, gq, resid, gains, hg, cos, sin, gg, ghq, *rest):
    bq, bkv = rest[:nf], rest[nf : 2 * nf]
    pay_o, grad_o, wq, wkv = rest[2 * nf :]
    f = f_ref[0]
    rows = tok.shape[0]
    assemble(f, bkv, wkv)
    assemble(f, bq, wq)
    u, r = unit(kraw[...])
    c = rotate_back(gkv[:, :HEAD_DIM], cos[...], sin[...])
    gk, ghk = norm_back(c, u, r, hg[1:2, :])
    gkl = gk.astype(BF)
    gvl = gkv[:, HEAD_DIM:].astype(BF)
    pay_o[:rows, :HEAD_DIM] = gkl
    pay_o[:rows, HEAD_DIM:] = gvl
    gn = dot_nt(gq[...], wq[...]) + dot_nt(gkl, wkv[:, :HEAD_DIM]) + dot_nt(gvl, wkv[:, HEAD_DIM:])
    u, r = unit(tok[...].astype(F32))
    gx, gain0 = norm_back(gn, u, r, gains[0:1, :])
    grad_o[...] = resid[...] + gx
    all_gains = jnp.concatenate([gain0, gg[...]], axis=0)
    wide = 2 * HEAD_DIM
    tail = jnp.concatenate([all_gains[i : i + 1, wide:] for i in range(4)], axis=1)
    heads = jnp.concatenate([ghq[...], ghk], axis=1)
    pad = jnp.zeros((10, wide), F32)
    pay_o[rows:, :] = jnp.concatenate([all_gains[:, :wide], tail, heads, pad], axis=0).astype(BF)


def ff_grad_kernel(nf, *refs):
    fg, ex = refs[:nf], refs[nf : 2 * nf]
    gu_o, down_o, fg_s, ex_s = refs[2 * nf :]
    rows = fg[0].shape[0]
    for k in range(nf):
        fg_s[k * rows : (k + 1) * rows, :] = fg[k][...]
        ex_s[k * rows : (k + 1) * rows, :] = ex[k][...]
    d = down_o.shape[1]
    width = down_o.shape[0]
    gu_o[...] = dot_tn(fg_s[:, :d], ex_s[:, width:]).astype(BF)
    down_o[...] = dot_tn(ex_s[:, :width], fg_s[:, d:]).astype(BF)


def pair_grad_kernel(nf, rows, *refs):
    a, b = refs[:nf], refs[nf : 2 * nf]
    outs, (a_s, b_s) = refs[2 * nf : -2], refs[-2:]
    for k in range(nf):
        a_s[k * rows : (k + 1) * rows, :] = a[k][...]
        b_s[k * rows : (k + 1) * rows, :] = b[k][:rows, :]
    outs[0][...] = dot_tn(a_s[...], b_s[...]).astype(BF)
    if len(outs) > 1:
        total = b[0][rows:, :].astype(F32)
        for k in range(1, nf):
            total = total + b[k][rows:, :].astype(F32)
        outs[1][...] = total.astype(BF)


def swap(x, axis, n, bit):
    return lax.ppermute(x, axis, [(i, i ^ bit) for i in range(n)])


def gather_xor(x, axis, n):
    have = {0: x}
    bit = n // 2
    while bit:
        for k in list(have):
            have[k | bit] = swap(have[k], axis, n, bit)
        bit //= 2
    return [have[k] for k in range(n)]


def exchange_xor(blocks, axis, n):
    return [b if k == 0 else swap(b, axis, n, k) for k, b in enumerate(blocks)]


def gather_ctx(x, n):
    if n > 8:
        bit = 1
        while bit < n:
            x = jnp.concatenate([x, swap(x, "ctx", n, bit)], axis=0)
            bit *= 2
        return x
    far = {0: x}
    for k in range(n - 2, 0, -2):
        far[k] = swap(x, "ctx", n, k)
    have = {}
    for k in sorted(far):
        have[k] = far[k]
        have[k + 1] = swap(far[k], "ctx", n, 1)
    return jnp.concatenate([have[k] for k in range(n)], axis=0)


def scatter_sum_ctx(x, n):
    rows = x.shape[0] // n
    if n > 8:
        bit = n // 2
        while bit:
            keep, send = x[: bit * rows], x[bit * rows :]
            got = swap(send, "ctx", n, bit)
            x = (keep.astype(F32) + got.astype(F32)).astype(BF)
            bit //= 2
        return x.astype(F32)
    blocks = [x[k * rows : (k + 1) * rows] for k in range(n)]
    got = {k: swap(blocks[k], "ctx", n, 1) for k in range(n - 1, 0, -2)}
    total = None
    for k in range(n - 2, -1, -2):
        part = blocks[k].astype(F32) + got[k + 1].astype(F32)
        if k:
            part = swap(part.astype(BF), "ctx", n, k).astype(F32)
        total = part if total is None else total + part
    return total


def sum_ctx(x, n, c, bits):
    if x.shape[0] % n:
        return lax.psum(x.astype(F32), "ctx")
    for bit in bits:
        half = x.shape[0] // 2
        upper = (c & bit) != 0
        keep = jnp.where(upper, x[half:], x[:half])
        send = jnp.where(upper, x[:half], x[half:])
        got = swap(send, "ctx", n, bit)
        x = (keep.astype(F32) + got.astype(F32)).astype(BF)
    for bit in reversed(bits):
        upper = (c & bit) != 0
        got = swap(x, "ctx", n, bit)
        x = jnp.concatenate([jnp.where(upper, got, x), jnp.where(upper, x, got)], axis=0)
    return x.astype(F32)


def sum_ctx_direct(x, gains, n, c):
    if n > 8 or x.shape[0] % n:
        return lax.psum(x.astype(F32), "ctx"), lax.psum(gains.astype(F32), "ctx")
    rows = x.shape[0] // n
    pieces = x.reshape(n, rows, x.shape[1])
    total = None
    for k in range(n):
        piece = lax.dynamic_index_in_dim(pieces, c ^ k, 0, keepdims=False)
        piece = jnp.concatenate([piece, gains], axis=0)
        if k:
            piece = swap(piece, "ctx", n, k)
        piece = piece.astype(F32)
        total = piece if total is None else total + piece
    mine = total[:rows].astype(BF)
    got = jnp.stack([mine] + [swap(mine, "ctx", n, k) for k in range(1, n)])
    got = jnp.take(got, c ^ jnp.arange(n), axis=0)
    return got.reshape(x.shape).astype(F32), total[rows:]


def layer(
    nf,
    nc,
    tokens,
    cotangent,
    block_order,
    query_weight,
    key_weight,
    value_weight,
    out_weight,
    gate_weight,
    up_weight,
    down_weight,
    norm_gains,
    head_gains,
):
    rows, d = tokens.shape
    block_len = rows // 2
    f = lax.axis_index("fsdp")
    c = lax.axis_index("ctx")
    f_arr = f.reshape(1).astype(jnp.int32)
    seq = nc * rows
    tile = min(seq, 1024)
    proj = HEADS * HEAD_DIM
    width = gate_weight.shape[1]

    gain_pack = jnp.concatenate([norm_gains.reshape(-1), head_gains.reshape(-1)]).reshape(-1, 128)
    gain_blocks = gather_xor(gain_pack, "fsdp", nf)
    wkv = gather_xor(jnp.concatenate([key_weight, value_weight], axis=1), "fsdp", nf)
    wq = gather_xor(query_weight, "fsdp", nf)
    wo = gather_xor(out_weight, "fsdp", nf)
    wg = gather_xor(gate_weight, "fsdp", nf)
    wu = gather_xor(up_weight, "fsdp", nf)
    wd = gather_xor(down_weight, "fsdp", nf)

    pack = jnp.stack(gain_blocks).reshape(nf, -1).astype(F32)
    pack = jnp.take(pack, f ^ jnp.arange(nf), axis=0)
    split = norm_gains.size
    gains = pack[:, :split].reshape(nf, 4, -1).transpose(1, 0, 2).reshape(4, d)
    hg = pack[:, split:].reshape(nf, 2, -1).transpose(1, 0, 2).reshape(2, HEAD_DIM)

    order = jnp.take(block_order.reshape(nc, 2), c ^ jnp.arange(nc), axis=0)
    kpos = (order.reshape(-1, 1) * block_len + jnp.arange(block_len)[None, :]).reshape(1, seq)
    qpos = kpos[0, :rows].reshape(rows, 1)
    inv_freq = ROPE_BASE ** (-2.0 * jnp.arange(HEAD_DIM // 2, dtype=F32) / HEAD_DIM)
    angles = qpos.astype(F32) * inv_freq[None, :]
    cos, sin = jnp.cos(angles), jnp.sin(angles)

    normed, kraw, kv = call(
        functools.partial(kv_kernel, nf),
        [((rows, d), BF), ((rows, HEAD_DIM), F32), ((rows, 2 * HEAD_DIM), BF)],
        f_arr, tokens, gains, hg, cos, sin, *wkv,
        scratch=[pltpu.VMEM((d, 2 * HEAD_DIM), BF)], smem_first=True,
        flops=2 * rows * d * 2 * HEAD_DIM,
    )
    kv_all = gather_ctx(kv, nc)
    qraw, q = call(
        functools.partial(query_kernel, nf),
        [((HEADS, rows, HEAD_DIM), F32), ((HEADS, rows, HEAD_DIM), BF)],
        f_arr, normed, hg, cos, sin, *wq,
        scratch=[pltpu.VMEM((d, proj), BF)], smem_first=True, flops=2 * rows * d * proj,
    )
    att, att_low, tot = call(
        functools.partial(attend_kernel, tile),
        [((HEADS, rows, HEAD_DIM), F32), ((HEADS, rows, HEAD_DIM), BF), ((HEADS, rows, 1), F32)],
        q, kv_all, hg, qpos, kpos, flops=4 * rows * proj * seq,
    )
    ff_outs = call(
        functools.partial(ff_kernel, nf),
        [
            ((rows, d), BF),
            ((rows, 2 * d), BF),
            ((rows, d), BF),
            ((rows, d), F32),
            ((3, d), F32),
        ]
        + [((rows, 3 * width), BF)] * nf,
        tokens, cotangent, gains, att_low, *wo, *wg, *wu, *wd,
        scratch=[pltpu.VMEM((nf, rows, width), F32)] * 2, flops=2 * rows * d * width * nf * 8,
    )
    output, fg, gbl, resid, gg = ff_outs[:5]
    ex = ff_outs[5:]

    fg_all = gather_xor(fg, "fsdp", nf)
    ex_all = exchange_xor(ex, "fsdp", nf)
    gq, ghq, gkv = call(
        functools.partial(attend_back_kernel, nf, tile),
        [((rows, proj), BF), ((1, HEAD_DIM), F32), ((seq, 2 * HEAD_DIM), BF)],
        f_arr, gbl, att, tot, q, qraw, kv_all, hg, cos, sin, qpos, kpos, *wo,
        scratch=[
            pltpu.VMEM((HEADS * rows, HEAD_DIM), BF),
            pltpu.VMEM((HEADS, rows, 1), F32),
            pltpu.VMEM((HEADS, rows, HEAD_DIM), F32),
            pltpu.VMEM((HEADS * rows, tile), BF),
            pltpu.VMEM((HEADS * rows, tile), BF),
        ],
        smem_first=True, flops=10 * rows * proj * seq,
    )
    gkv_own = scatter_sum_ctx(gkv, nc)

    gu_part, down_part = call(
        functools.partial(ff_grad_kernel, nf),
        [((d, 2 * width), BF), ((width, d), BF)],
        *fg_all, *ex_all,
        scratch=[pltpu.VMEM((nf * rows, 2 * d), BF), pltpu.VMEM((nf * rows, 3 * width), BF)],
        flops=6 * nf * rows * d * width,
    )
    up_bits = [1 << i for i in range(nc.bit_length() - 1)]
    alt_bits = up_bits[1:2] + up_bits[:1] + up_bits[2:]
    gu = sum_ctx(gu_part, nc, c, up_bits)
    grad_down = sum_ctx(down_part, nc, c, alt_bits)

    def pair_grad(a, b, shape, extra=()):
        return call(
            functools.partial(pair_grad_kernel, nf, rows),
            [(shape, BF)] + list(extra),
            *a, *b,
            scratch=[
                pltpu.VMEM((nf * rows, shape[0]), BF),
                pltpu.VMEM((nf * rows, shape[1]), BF),
            ],
            flops=2 * nf * rows * shape[0] * shape[1],
        )

    att_cols = exchange_xor([att_low[k] for k in range(nf)], "fsdp", nf)
    gbl_all = gather_xor(gbl, "fsdp", nf)
    (out_part,) = pair_grad(att_cols, gbl_all, (proj // nf, d))
    grad_out = sum_ctx(out_part, nc, c, alt_bits)

    share = d // nf
    cols = exchange_xor(
        [lax.dynamic_slice_in_dim(normed, (f ^ k) * share, share, 1) for k in range(nf)], "fsdp", nf
    )
    gq_all = gather_xor(gq, "fsdp", nf)
    (q_part,) = pair_grad(cols, gq_all, (share, proj))
    grad_q = sum_ctx(q_part, nc, c, up_bits)

    pay, input_grad = call(
        functools.partial(input_back_kernel, nf),
        [((rows + 16, 2 * HEAD_DIM), BF), ((rows, d), F32)],
        f_arr, tokens, gkv_own, kraw, gq, resid, gains, hg, cos, sin, gg, ghq, *wq, *wkv,
        scratch=[pltpu.VMEM((d, proj), BF), pltpu.VMEM((d, 2 * HEAD_DIM), BF)],
        smem_first=True, flops=2 * rows * d * (proj + 2 * HEAD_DIM),
    )
    pay_all = gather_xor(pay, "fsdp", nf)
    kv_part, gain_part = pair_grad(
        cols, pay_all, (share, 2 * HEAD_DIM), [((16, 2 * HEAD_DIM), BF)]
    )
    grad_kv, gain_sum = sum_ctx_direct(kv_part, gain_part, nc, c)

    wide = 2 * HEAD_DIM
    norm_sum = jnp.concatenate([gain_sum[:4], gain_sum[4].reshape(4, -1)], axis=1)
    head_sum = gain_sum[5].reshape(2, HEAD_DIM)
    grad_gains = lax.dynamic_slice_in_dim(norm_sum, f * share, share, 1)
    grad_heads = lax.dynamic_slice_in_dim(head_sum, f * (HEAD_DIM // nf), HEAD_DIM // nf, 1)
    return (
        output,
        input_grad,
        grad_q,
        grad_kv[:, :HEAD_DIM],
        grad_kv[:, HEAD_DIM:],
        grad_out,
        gu[:, :width],
        gu[:, width:],
        grad_down,
        grad_gains,
        grad_heads,
    )


def solution(mesh):
    row = P(("ctx", "fsdp"), None)
    first, second = P("fsdp", None), P(None, "fsdp")
    body = functools.partial(layer, mesh.shape["fsdp"], mesh.shape["ctx"])
    return jax.shard_map(
        body,
        mesh=mesh,
        in_specs=(row, row, P(), first, first, first, first, second, second, first, second, second),
        out_specs=(row, row, first, first, first, first, second, second, first, second, second),
        check_vma=False,
    )
```

```python
import functools
import math

import jax
import jax.numpy as jnp
from jax import lax
from jax.experimental import pallas as pl
from jax.experimental.pallas import tpu as pltpu
from jax.sharding import PartitionSpec as P

HEADS = 4
HEAD_DIM = 256
NORM_EPS = 1e-06
ROPE_BASE = 1000000.0
BF = jnp.bfloat16
F32 = jnp.float32
MIB = 1024 * 1024


def dot(a, b):
    return lax.dot_general(a, b, (((1,), (0,)), ((), ())), preferred_element_type=F32)


def dot_nt(a, b):
    return lax.dot_general(a, b, (((1,), (1,)), ((), ())), preferred_element_type=F32)


def dot_tn(a, b):
    return lax.dot_general(a, b, (((0,), (0,)), ((), ())), preferred_element_type=F32)


def unit(v):
    r = lax.rsqrt(jnp.mean(v * v, axis=-1, keepdims=True) + NORM_EPS)
    return v * r, r


def norm_back(c, u, r, g):
    cg = c * g
    grad = r * (cg - u * jnp.mean(cg * u, axis=-1, keepdims=True))
    return grad, jnp.sum(c * u, axis=0, keepdims=True)


def rotate(v, cos, sin):
    half = v.shape[-1] // 2
    a, b = v[:, :half], v[:, half:]
    return jnp.concatenate([a * cos - b * sin, b * cos + a * sin], axis=-1)


def rotate_back(v, cos, sin):
    half = v.shape[-1] // 2
    a, b = v[:, :half], v[:, half:]
    return jnp.concatenate([a * cos + b * sin, b * cos - a * sin], axis=-1)


def call(kernel, outs, *args, scratch=(), vmem=40, flops=0, smem_first=False):
    specs = [pl.BlockSpec(memory_space=pltpu.VMEM)] * len(args)
    if smem_first:
        specs[0] = pl.BlockSpec(memory_space=pltpu.SMEM)
    moved = sum(math.prod(a.shape) * a.dtype.itemsize for a in args)
    return pl.pallas_call(
        kernel,
        out_shape=[jax.ShapeDtypeStruct(s, d) for s, d in outs],
        in_specs=specs,
        out_specs=[pl.BlockSpec(memory_space=pltpu.VMEM)] * len(outs),
        scratch_shapes=list(scratch),
        compiler_params=pltpu.CompilerParams(vmem_limit_bytes=vmem * MIB),
        cost_estimate=pl.CostEstimate(flops=flops, bytes_accessed=moved, transcendentals=0),
    )(*args)


def bound_of(hg):
    peak = jnp.max(jnp.abs(hg[...]), axis=1, keepdims=True)
    return math.sqrt(HEAD_DIM) * peak[0:1, :] * peak[1:2, :]


def tile_loop(count, step):
    if count == 1:
        step(0)
    else:

        def body(t, carry):
            step(t)
            return carry

        lax.fori_loop(0, count, body, 0)


def tile_rows(t, tile, count):
    return pl.ds(pl.multiple_of(t * tile, tile), tile) if count > 1 else slice(None)


def front_kernel(nf, tile, f_ref, tok, gains, hg, cos, sin, qpos, kpos, *rest):
    blocks = rest[:nf]
    normed_o, kraw_o, kv_o, qraw_o, q_o, att_o, low_o, tot_o, w = rest[nf:]
    f = f_ref[0]
    share = w.shape[0] // nf
    rows = qpos.shape[0]
    proj = HEADS * HEAD_DIM
    scale = 1.0 / math.sqrt(HEAD_DIM)
    count = tok.shape[0] // tile
    bound = bound_of(hg)
    for k in range(nf):
        start = pl.multiple_of(jnp.bitwise_xor(f, k) * share, 16)
        w[pl.ds(start, share), :] = blocks[k][:share, :]

    def keys(t):
        part = tile_rows(t, tile, count)
        u, _ = unit(tok[part, :].astype(F32))
        normed = (u * gains[0:1, :]).astype(BF)
        normed_o[part, :] = normed
        out = dot(normed, w[:, proj:])
        key = out[:, :HEAD_DIM]
        kraw_o[part, :] = key
        u, _ = unit(key)
        kv_o[part, :HEAD_DIM] = rotate(u * hg[1:2, :], cos[part, :], sin[part, :]).astype(BF)
        kv_o[part, HEAD_DIM:] = out[:, HEAD_DIM:].astype(BF)

    tile_loop(count, keys)
    for h in range(HEADS):
        raw = dot(normed_o[:rows, :], w[:, h * HEAD_DIM : (h + 1) * HEAD_DIM])
        k = jnp.bitwise_xor(f, h)
        qraw_o[k] = raw
        u, _ = unit(raw)
        q_o[k] = rotate(u * hg[0:1, :], cos[:rows, :], sin[:rows, :]).astype(BF)
    for k in range(HEADS):

        def step(t, k=k):
            part = tile_rows(t, tile, count)
            raw = dot_nt(q_o[k], kv_o[part, :HEAD_DIM])
            allowed = kpos[:, part] <= qpos[...]
            terms = jnp.where(allowed, jnp.exp(raw * scale - bound), 0.0)
            total = jnp.sum(terms, axis=1, keepdims=True)
            num = dot(terms.astype(BF), kv_o[part, HEAD_DIM:])
            if count == 1:
                tot_o[k], att_o[k] = total, num
            else:
                tot_o[k] += total
                att_o[k] += num

        if count > 1:
            tot_o[k] = jnp.zeros_like(tot_o[k])
            att_o[k] = jnp.zeros_like(att_o[k])
        tile_loop(count, step)
        att = att_o[k] / tot_o[k]
        att_o[k] = att
        low_o[k] = att.astype(BF)


def mid_kernel(nf, tok, gains, att, *rest):
    wo = rest[:nf]
    branch_o, middle_o, ff_o = rest[nf:]
    branch = None
    for k in range(nf):
        term = dot(att[k], wo[k][...])
        branch = term if branch is None else branch + term
    branch_o[...] = branch
    u, _ = unit(branch)
    middle = tok[...].astype(F32) + u * gains[1:2, :]
    middle_o[...] = middle
    u, _ = unit(middle)
    ff_o[...] = (u * gains[2:3, :]).astype(BF)


def gelu_parts(v):
    t = jnp.tanh(0.7978845608028654 * (v + 0.044715 * v * v * v))
    half = 0.5 * (1.0 + t)
    slope = half + 0.5 * v * (1.0 - t * t) * 0.7978845608028654 * (1.0 + 3 * 0.044715 * v * v)
    return v * half, slope


def ff_kernel(mine, other, wg0, wu0, wd0, wg1, wu1, wd1, own_o, send_o, pack_o, hid_o, a_o, b_o):
    rows, d = mine.shape
    pack_o[:rows, :d] = mine[...]
    pack_o[rows:, :d] = other[...]
    x = pack_o[:, :d]
    mixed = None
    for i, (wg, wu, wd) in enumerate(((wg0, wu0, wd0), (wg1, wu1, wd1))):
        gate = dot(x, wg[...])
        up = dot(x, wu[...])
        value, slope = gelu_parts(gate)
        a_o[i] = value
        b_o[i] = up * slope
        hidden = (value * up).astype(BF)
        if i == 0:
            hid_o[...] = hidden
        else:
            pack_o[:, d:] = hidden
        term = dot(hidden, wd[...])
        mixed = term if mixed is None else mixed + term
    own_o[...] = mixed[:rows, :]
    send_o[...] = mixed[rows:, :].astype(BF)


def finish_kernel(own, got, middle, cot, gains, out_o, low_o, gain_o):
    u, r = unit(own[...] + got[...].astype(F32))
    out_o[...] = (middle[...] + u * gains[3:4, :]).astype(BF)
    grad, gain = norm_back(cot[...].astype(F32), u, r, gains[3:4, :])
    low_o[...] = grad.astype(BF)
    gain_o[...] = gain


def ff_back_kernel(
    mine, other, a, b, wg0, wu0, wd0, wg1, wu1, wd1, own_o, send_o, pack_o, gg_o
):
    rows, d = mine.shape
    width = wg0.shape[1]
    pack_o[:rows, :d] = mine[...]
    pack_o[rows:, :d] = other[...]
    c = pack_o[:, :d]
    total = None
    for i, (wg, wu, wd) in enumerate(((wg0, wu0, wd0), (wg1, wu1, wd1))):
        gh = dot_nt(c, wd[...])
        gg = (gh * b[i]).astype(BF)
        gu = (gh * a[i]).astype(BF)
        if i == 0:
            gg_o[:, :width] = gg
            gg_o[:, width:] = gu
        else:
            pack_o[:, d : d + width] = gg
            pack_o[:, d + width :] = gu
        term = dot_nt(gg, wg[...]) + dot_nt(gu, wu[...])
        total = term if total is None else total + term
    own_o[...] = total[:rows, :]
    send_o[...] = total[rows:, :].astype(BF)


def ff_grad_kernel(pack1, hid, got1, pack2, gg, got2, gu_o, down_o, x_s, h_s, c_s, g_s):
    rows = hid.shape[0]
    d = down_o.shape[1]
    width = down_o.shape[0]
    x_s[:rows, :] = pack1[:, :d]
    x_s[rows:, :] = got1[:, :d]
    h_s[:rows, :] = hid[...]
    h_s[rows:, :] = got1[:, d:]
    c_s[:rows, :] = pack2[:, :d]
    c_s[rows:, :] = got2[:, :d]
    g_s[:rows, :] = gg[...]
    g_s[rows:, :] = got2[:, d:]
    gu_o[...] = dot_tn(x_s[...], g_s[...]).astype(BF)
    down_o[...] = dot_tn(h_s[...], c_s[...]).astype(BF)


def back_kernel(
    nf, tile, f_ref, own, got, middle, branch, cot, gains, gain3, att, tot, q, qraw, kv, normed,
    kraw, hg, cos, sin, qpos, kpos, *rest,
):
    wo = rest[:nf]
    pack_o, resid_o, odd_o, even_o = rest[nf : nf + 4]
    kvw_o = rest[nf + 4 : 2 * nf + 4]
    sg_s, tg_s, acc, s_s, e_s, kvw_s = rest[2 * nf + 4 :]
    f = f_ref[0]
    scale = 1.0 / math.sqrt(HEAD_DIM)
    rows, d = cot.shape
    proj = HEADS * HEAD_DIM
    bound = bound_of(hg)
    count = kv.shape[0] // tile
    um, rm = unit(middle[...])
    grad, gain2 = norm_back(own[...] + got[...].astype(F32), um, rm, gains[2:3, :])
    grad_middle = cot[...].astype(F32) + grad
    resid_o[...] = grad_middle
    ub, rb = unit(branch[...])
    grad_branch, gain1 = norm_back(grad_middle, ub, rb, gains[1:2, :])
    gbl = grad_branch.astype(BF)
    pack_o[:rows, proj:] = gbl
    for k in range(HEADS):
        ga = dot_nt(gbl, wo[k][...])
        inv = 1.0 / tot[k]
        sg_s[k * rows : (k + 1) * rows, :] = (ga * inv).astype(BF)
        tg_s[k] = -jnp.sum(ga * att[k], axis=1, keepdims=True) * inv

    def step(t):
        part = tile_rows(t, tile, count)
        allowed = kpos[:, part] <= qpos[...]
        for k in range(HEADS):
            mine = slice(k * rows, (k + 1) * rows)
            raw = dot_nt(q[k], kv[part, :HEAD_DIM])
            terms = jnp.where(allowed, jnp.exp(raw * scale - bound), 0.0)
            e_s[mine, :] = terms.astype(BF)
            gp = dot_nt(sg_s[mine, :], kv[part, HEAD_DIM:])
            s = (terms * (gp + tg_s[k]) * scale).astype(BF)
            s_s[mine, :] = s
            term = dot(s, kv[part, :HEAD_DIM])
            if count == 1:
                acc[k] = term
            else:
                acc[k] += term
        queries = q[...].reshape(HEADS * rows, HEAD_DIM)
        c = rotate_back(dot_tn(s_s[...], queries), cos[part, :], sin[part, :])
        u, r = unit(kraw[part, :])
        gk, gain = norm_back(c, u, r, hg[1:2, :])
        gkl = gk.astype(BF)
        gvl = dot_tn(e_s[...], sg_s[...]).astype(BF)
        kk = dot_tn(normed[part, :], gkl)
        vv = dot_tn(normed[part, :], gvl)
        if count == 1:
            kvw_s[:d, :HEAD_DIM] = kk
            kvw_s[:d, HEAD_DIM:] = vv
            kvw_s[d : d + 1, :HEAD_DIM] = gain
        else:
            kvw_s[:d, :HEAD_DIM] += kk
            kvw_s[:d, HEAD_DIM:] += vv
            kvw_s[d : d + 1, :HEAD_DIM] += gain
        for j in range(tile // rows):
            out = even_o if j % 2 == 0 else odd_o
            start = (j // 2) * rows
            if count > 1:
                start = pl.multiple_of(t * (tile // 2) + start, rows)
            out[pl.ds(start, rows), :HEAD_DIM] = gkl[j * rows : (j + 1) * rows, :]
            out[pl.ds(start, rows), HEAD_DIM:] = gvl[j * rows : (j + 1) * rows, :]

    if count > 1:
        acc[...] = jnp.zeros_like(acc)
        kvw_s[...] = jnp.zeros_like(kvw_s)
    tile_loop(count, step)
    share = kvw_o[0].shape[0]
    for k in range(nf):
        start = pl.multiple_of(jnp.bitwise_xor(f, k) * share, 16)
        kvw_o[k][...] = kvw_s[pl.ds(start, share), :].astype(BF)
    gain = None
    for k in range(HEADS):
        u, r = unit(qraw[k])
        c = rotate_back(acc[k], cos[:rows, :], sin[:rows, :])
        grad, g = norm_back(c, u, r, hg[0:1, :])
        gain = g if gain is None else gain + g
        h = jnp.bitwise_xor(f, k)
        pack_o[:rows, pl.ds(pl.multiple_of(h * HEAD_DIM, HEAD_DIM), HEAD_DIM)] = grad.astype(BF)
    wide = pack_o.shape[1]
    first = jnp.concatenate([gain1, gain2, jnp.zeros((1, wide - 2 * d), F32)], axis=1)
    heads = jnp.concatenate([gain, kvw_s[d : d + 1, :HEAD_DIM]], axis=1)
    second = jnp.concatenate(
        [gain3[...], heads, jnp.zeros((1, wide - d - 2 * HEAD_DIM), F32)], axis=1
    )
    pad = jnp.zeros((pack_o.shape[0] - rows - 2, wide), F32)
    pack_o[rows:, :] = jnp.concatenate([first, second, pad], axis=0).astype(BF)


def attention_grad_kernel(nf, *refs):
    pack, cols, kvw = refs[:nf], refs[nf : 2 * nf], refs[2 * nf : 3 * nf]
    out_o, gain_o, g_s, b_s, a_s, n_s = refs[3 * nf :]
    rows = cols[0].shape[0]
    proj = HEADS * HEAD_DIM
    head = a_s.shape[1]
    share = n_s.shape[1]
    for k in range(nf):
        mine = slice(k * rows, (k + 1) * rows)
        g_s[mine, :] = pack[k][:rows, :proj]
        b_s[mine, :] = pack[k][:rows, proj:]
        a_s[mine, :] = cols[k][:, :head]
        n_s[mine, :] = cols[k][:, head : head + share]
    qw = dot_tn(n_s[...], g_s[...])
    half = proj // 2
    out_o[:share, :] = qw[:, :half].astype(BF)
    out_o[share : 2 * share, :] = qw[:, half:].astype(BF)
    total = kvw[0][...].astype(F32)
    gain = pack[0][rows:, :].astype(F32)
    for k in range(1, nf):
        total = total + kvw[k][...].astype(F32)
        gain = gain + pack[k][rows:, :].astype(F32)
    out_o[2 * share : 3 * share, :] = total.astype(BF)
    gain_o[...] = gain.astype(BF)
    ow = dot_tn(a_s[...], b_s[...])
    at = 3 * share
    out_o[at : at + head, :] = ow[:, :half].astype(BF)
    at += head
    quarter = head // 4
    strip = jnp.concatenate(
        [ow[i * quarter : (i + 1) * quarter, half:] for i in range(4)], axis=1
    )
    out_o[at : at + quarter, :] = strip.astype(BF)
    at += quarter
    out_o[at:, :] = jnp.zeros((out_o.shape[0] - at, half), BF)


def input_back_kernel(nf, f_ref, tok, gkv, pack, resid, gains, *rest):
    blocks, (grad_o, w) = rest[:nf], rest[nf:]
    f = f_ref[0]
    rows = tok.shape[0]
    share = w.shape[0] // nf
    proj = HEADS * HEAD_DIM
    for k in range(nf):
        start = pl.multiple_of(jnp.bitwise_xor(f, k) * share, 16)
        w[pl.ds(start, share), :] = blocks[k][:share, :]
    low = gkv[...].astype(BF)
    gn = dot_nt(pack[:rows, :proj], w[:, :proj]) + dot_nt(low, w[:, proj:])
    u, r = unit(tok[...].astype(F32))
    gx, _ = norm_back(gn, u, r, gains[0:1, :])
    grad_o[...] = resid[...] + gx


def swap(x, axis, n, bit):
    return lax.ppermute(x, axis, [(i, i ^ bit) for i in range(n)])


def gather_fsdp(x, n):
    far = swap(x, "fsdp", n, 2)
    both = swap(jnp.concatenate([x, far], axis=0), "fsdp", n, 1)
    rows = x.shape[0]
    return [x, both[:rows], far, both[rows:]]


def exchange_fsdp(blocks, n):
    return [b if k == 0 else swap(b, "fsdp", n, k) for k, b in enumerate(blocks)]


def gather_ctx(x, n):
    if n > 8:
        bit = 1
        while bit < n:
            x = jnp.concatenate([x, swap(x, "ctx", n, bit)], axis=0)
            bit *= 2
        return x
    far = {0: x}
    for k in range(n - 2, 0, -2):
        far[k] = swap(x, "ctx", n, k)
    have = {}
    for k in sorted(far):
        have[k] = far[k]
        have[k + 1] = swap(far[k], "ctx", n, 1)
    return jnp.concatenate([have[k] for k in range(n)], axis=0)


def scatter_sum_ctx(odd, even, n):
    x = even.astype(F32) + swap(odd, "ctx", n, 1).astype(F32)
    rows = x.shape[0] * 2 // n
    if n > 8:
        bit = n // 2
        while bit > 1:
            half = x.shape[0] // 2
            x = x[:half] + swap(x[half:].astype(BF), "ctx", n, bit).astype(F32)
            bit //= 2
        return x
    total = x[:rows]
    for k in range(n // 2 - 1, 0, -1):
        part = x[k * rows : (k + 1) * rows].astype(BF)
        total = total + swap(part, "ctx", n, 2 * k).astype(F32)
    return total


def sum_ctx(x, n, c, bits):
    if x.shape[0] % n:
        return lax.psum(x.astype(F32), "ctx")
    for bit in bits:
        half = x.shape[0] // 2
        upper = (c & bit) != 0
        keep = jnp.where(upper, x[half:], x[:half])
        send = jnp.where(upper, x[:half], x[half:])
        got = swap(send, "ctx", n, bit)
        x = (keep.astype(F32) + got.astype(F32)).astype(BF)
    for bit in reversed(bits):
        upper = (c & bit) != 0
        got = swap(x, "ctx", n, bit)
        x = jnp.concatenate([jnp.where(upper, got, x), jnp.where(upper, x, got)], axis=0)
    return x.astype(F32)


def sum_small(x, n):
    x = x.astype(F32)
    bit = 1
    while bit < n:
        x = x + swap(x.astype(BF), "ctx", n, bit).astype(F32)
        bit *= 2
    return x


def layer(
    nf,
    nc,
    tokens,
    cotangent,
    block_order,
    query_weight,
    key_weight,
    value_weight,
    out_weight,
    gate_weight,
    up_weight,
    down_weight,
    norm_gains,
    head_gains,
):
    rows, d = tokens.shape
    block_len = rows // 2
    f = lax.axis_index("fsdp")
    c = lax.axis_index("ctx")
    f_arr = f.reshape(1).astype(jnp.int32)
    seq = nc * rows
    tile = min(seq, 1024)
    proj = HEADS * HEAD_DIM
    width = gate_weight.shape[1]
    share = d // nf
    qkv = proj + 2 * HEAD_DIM
    hd = (HEADS, rows, HEAD_DIM)

    pack = jnp.concatenate([norm_gains.reshape(1, -1), head_gains.reshape(1, -1)], axis=1)
    pack = jnp.pad(pack, ((0, 15), (0, qkv - pack.shape[1])))
    weights = jnp.concatenate([query_weight, key_weight, value_weight], axis=1)
    wqkv = gather_fsdp(jnp.concatenate([weights, pack], axis=0), nf)
    tok_all = gather_ctx(tokens, nc)
    wo = gather_fsdp(out_weight, nf)
    own_ff = (gate_weight, up_weight, down_weight)
    next_ff = [swap(w, "fsdp", nf, 1) for w in own_ff]

    split = norm_gains.size
    rest = split + head_gains.size
    pack = jnp.concatenate([w[share : share + 1, :rest] for w in wqkv], axis=0).astype(F32)
    pack = jnp.take(pack, f ^ jnp.arange(nf), axis=0)
    gains = pack[:, :split].reshape(nf, 4, -1).transpose(1, 0, 2).reshape(4, d)
    hg = pack[:, split:].reshape(nf, 2, -1).transpose(1, 0, 2).reshape(2, HEAD_DIM)

    order = jnp.take(block_order.reshape(nc, 2), c ^ jnp.arange(nc), axis=0)
    pos = (order.reshape(-1, 1) * block_len + jnp.arange(block_len)[None, :]).reshape(seq)
    kpos = pos.reshape(1, seq)
    qpos = pos[:rows].reshape(rows, 1)
    inv_freq = ROPE_BASE ** (-2.0 * jnp.arange(HEAD_DIM // 2, dtype=F32) / HEAD_DIM)
    angles = pos.astype(F32)[:, None] * inv_freq[None, :]
    cos, sin = jnp.cos(angles), jnp.sin(angles)

    normed, kraw, kv, qraw, q, att, att_low, tot = call(
        functools.partial(front_kernel, nf, tile),
        [
            ((seq, d), BF), ((seq, HEAD_DIM), F32), ((seq, 2 * HEAD_DIM), BF),
            (hd, F32), (hd, BF), (hd, F32), (hd, BF), ((HEADS, rows, 1), F32),
        ],
        f_arr, tok_all, gains, hg, cos, sin, qpos, kpos, *wqkv,
        scratch=[pltpu.VMEM((d, qkv), BF)], smem_first=True, vmem=60,
        flops=4 * rows * proj * seq + 2 * seq * d * qkv,
    )
    branch, middle, ff_in = call(
        functools.partial(mid_kernel, nf),
        [((rows, d), F32), ((rows, d), F32), ((rows, d), BF)],
        tokens, gains, att_low, *wo, flops=2 * rows * d * proj,
    )
    cols = exchange_fsdp(
        [
            jnp.concatenate(
                [att_low[k], lax.dynamic_slice_in_dim(normed[:rows], (f ^ k) * share, share, 1)],
                axis=1,
            )
            for k in range(nf)
        ],
        nf,
    )
    two = 2 * rows
    own, send, pack1, hid, act, slope = call(
        ff_kernel,
        [
            ((rows, d), F32), ((rows, d), BF), ((two, d + width), BF), ((two, width), BF),
            ((2, two, width), F32), ((2, two, width), F32),
        ],
        ff_in, swap(ff_in, "fsdp", nf, 2), *own_ff, *next_ff, flops=6 * two * d * width * 2,
    )
    got1 = swap(pack1, "fsdp", nf, 1)
    output, gml, gain3 = call(
        finish_kernel,
        [((rows, d), BF), ((rows, d), BF), ((1, d), F32)],
        own, swap(send, "fsdp", nf, 2), middle, cotangent, gains,
    )
    own, send, pack2, gg = call(
        ff_back_kernel,
        [((rows, d), F32), ((rows, d), BF), ((two, d + 2 * width), BF), ((two, 2 * width), BF)],
        gml, swap(gml, "fsdp", nf, 2), act, slope, *own_ff, *next_ff,
        flops=6 * two * d * width * 2,
    )
    got2 = swap(pack2, "fsdp", nf, 1)
    back = call(
        functools.partial(back_kernel, nf, tile),
        [
            ((rows + 16, proj + d), BF),
            ((rows, d), F32),
            ((seq // 2, 2 * HEAD_DIM), BF),
            ((seq // 2, 2 * HEAD_DIM), BF),
        ]
        + [((share, 2 * HEAD_DIM), BF)] * nf,
        f_arr, own, swap(send, "fsdp", nf, 2), middle, branch, cotangent, gains, gain3, att, tot,
        q, qraw, kv, normed, kraw, hg, cos, sin, qpos, kpos, *wo,
        scratch=[
            pltpu.VMEM((HEADS * rows, HEAD_DIM), BF),
            pltpu.VMEM((HEADS, rows, 1), F32),
            pltpu.VMEM(hd, F32),
            pltpu.VMEM((HEADS * rows, tile), BF),
            pltpu.VMEM((HEADS * rows, tile), BF),
            pltpu.VMEM((d + 8, 2 * HEAD_DIM), F32),
        ],
        smem_first=True, vmem=60, flops=10 * rows * proj * seq,
    )
    pack3, resid, odd, even = back[:4]
    kvw = exchange_fsdp(back[4:], nf)
    pack_all = gather_fsdp(pack3, nf)
    gkv = scatter_sum_ctx(odd, even, nc)

    gu_part, down_part = call(
        ff_grad_kernel,
        [((d, 2 * width), BF), ((width, d), BF)],
        pack1, hid, got1, pack2, gg, got2,
        scratch=[
            pltpu.VMEM((2 * two, d), BF),
            pltpu.VMEM((2 * two, width), BF),
            pltpu.VMEM((2 * two, d), BF),
            pltpu.VMEM((2 * two, 2 * width), BF),
        ],
        flops=12 * two * d * width,
    )
    up_bits = [1 << i for i in range(nc.bit_length() - 1)]
    alt_bits = up_bits[1:2] + up_bits[:1] + up_bits[2:]
    gu = sum_ctx(gu_part, nc, c, up_bits)
    grad_down = sum_ctx(down_part, nc, c, alt_bits)

    (input_grad,) = call(
        functools.partial(input_back_kernel, nf),
        [((rows, d), F32)],
        f_arr, tokens, gkv, pack3, resid, gains, *wqkv,
        scratch=[pltpu.VMEM((d, qkv), BF)], smem_first=True, flops=2 * rows * d * qkv,
    )

    head = proj // nf
    half = proj // 2
    used = 3 * share + head + head // 4
    lines = -(-used // 128) * 128
    att_part, gain_part = call(
        functools.partial(attention_grad_kernel, nf),
        [((lines, half), BF), ((16, proj + d), BF)],
        *pack_all, *cols, *kvw,
        scratch=[
            pltpu.VMEM((nf * rows, proj), BF),
            pltpu.VMEM((nf * rows, d), BF),
            pltpu.VMEM((nf * rows, head), BF),
            pltpu.VMEM((nf * rows, share), BF),
        ],
        flops=2 * nf * rows * share * (proj + d),
    )
    total = sum_ctx(att_part, nc, c, alt_bits)
    gain_sum = sum_small(gain_part, nc)
    grad_q = jnp.concatenate([total[:share], total[share : 2 * share]], axis=1)
    grad_kv = total[2 * share : 3 * share]
    at = 3 * share
    strip = total[at + head : at + head + head // 4]
    piece = strip.shape[1] // 4
    strip = jnp.concatenate([strip[:, i * piece : (i + 1) * piece] for i in range(4)], axis=0)
    grad_out = jnp.concatenate([total[at : at + head], strip], axis=1)
    gain0 = jnp.sum(grad_q * query_weight.astype(F32), axis=1)
    gain0 += jnp.sum(
        grad_kv * jnp.concatenate([key_weight, value_weight], axis=1).astype(F32), axis=1
    )
    gain0 = gain0 / norm_gains[0].astype(F32)
    others = jnp.concatenate(
        [gain_sum[0:1, :d], gain_sum[0:1, d : 2 * d], gain_sum[1:2, :d]], axis=0
    )
    others = lax.dynamic_slice_in_dim(others, f * share, share, 1)
    heads = gain_sum[1, d : d + 2 * HEAD_DIM].reshape(2, HEAD_DIM)
    return (
        output,
        input_grad,
        grad_q,
        grad_kv[:, :HEAD_DIM],
        grad_kv[:, HEAD_DIM:],
        grad_out,
        gu[:, :width],
        gu[:, width:],
        grad_down,
        jnp.concatenate([gain0[None, :], others], axis=0),
        lax.dynamic_slice_in_dim(heads, f * (HEAD_DIM // nf), HEAD_DIM // nf, 1),
    )


def solution(mesh):
    row = P(("ctx", "fsdp"), None)
    first, second = P("fsdp", None), P(None, "fsdp")
    body = functools.partial(layer, mesh.shape["fsdp"], mesh.shape["ctx"])
    return jax.shard_map(
        body,
        mesh=mesh,
        in_specs=(row, row, P(), first, first, first, first, second, second, first, second, second),
        out_specs=(row, row, first, first, first, first, second, second, first, second, second),
        check_vma=False,
    )
```

```python
import functools
import math

import jax
import jax.numpy as jnp
from jax import lax
from jax.experimental import pallas as pl
from jax.experimental.pallas import tpu as pltpu
from jax.sharding import PartitionSpec as P

HEADS = 4
HEAD_DIM = 256
NORM_EPS = 1e-06
ROPE_BASE = 1000000.0
BF = jnp.bfloat16
F32 = jnp.float32
MIB = 1024 * 1024


def dot(a, b):
    return lax.dot_general(a, b, (((1,), (0,)), ((), ())), preferred_element_type=F32)


def dot_nt(a, b):
    return lax.dot_general(a, b, (((1,), (1,)), ((), ())), preferred_element_type=F32)


def dot_tn(a, b):
    return lax.dot_general(a, b, (((0,), (0,)), ((), ())), preferred_element_type=F32)


def unit(v):
    r = lax.rsqrt(jnp.mean(v * v, axis=-1, keepdims=True) + NORM_EPS)
    return v * r, r


def norm_back(c, u, r, g):
    cg = c * g
    grad = r * (cg - u * jnp.mean(cg * u, axis=-1, keepdims=True))
    return grad, jnp.sum(c * u, axis=0, keepdims=True)


def rotate(v, cos, sin):
    half = v.shape[-1] // 2
    a, b = v[:, :half], v[:, half:]
    return jnp.concatenate([a * cos - b * sin, b * cos + a * sin], axis=-1)


def rotate_back(v, cos, sin):
    half = v.shape[-1] // 2
    a, b = v[:, :half], v[:, half:]
    return jnp.concatenate([a * cos + b * sin, b * cos - a * sin], axis=-1)


def call(kernel, outs, *args, scratch=(), vmem=20, us=1.0, smem=0, after=()):
    specs = [pl.BlockSpec(memory_space=pltpu.VMEM)] * len(args)
    for i in range(smem):
        specs[i] = pl.BlockSpec(memory_space=pltpu.SMEM)
    specs += [pl.BlockSpec(memory_space=pl.ANY)] * len(after)
    moved = sum(math.prod(a.shape) * a.dtype.itemsize for a in args)
    used, skip = len(args), len(args) + len(after)

    def body(*refs):
        kernel(*refs[:used], *refs[skip:])

    return pl.pallas_call(
        body,
        out_shape=[jax.ShapeDtypeStruct(s, d) for s, d in outs],
        in_specs=specs,
        out_specs=[pl.BlockSpec(memory_space=pltpu.VMEM)] * len(outs),
        scratch_shapes=list(scratch),
        compiler_params=pltpu.CompilerParams(vmem_limit_bytes=vmem * MIB),
        cost_estimate=pl.CostEstimate(
            flops=int(us * 1.1e9), bytes_accessed=moved, transcendentals=0
        ),
    )(*args, *after)


def bound_of(hg):
    peak = jnp.max(jnp.abs(hg[...]), axis=1, keepdims=True)
    return math.sqrt(HEAD_DIM) * peak[0:1, :] * peak[1:2, :]


def tile_loop(count, step):
    if count == 1:
        step(0)
    else:

        def body(t, carry):
            step(t)
            return carry

        lax.fori_loop(0, count, body, 0)


def tile_rows(t, tile, count):
    return pl.ds(pl.multiple_of(t * tile, tile), tile) if count > 1 else slice(None)


def pack_kernel(wk, wv, ng, hg, out):
    share = wk.shape[0]
    out[:share, :HEAD_DIM] = wk[...]
    out[:share, HEAD_DIM:] = wv[...]
    tail = jnp.concatenate(
        [
            ng[...].astype(F32),
            jnp.concatenate(
                [hg[...].astype(F32), jnp.zeros((2, share - hg.shape[1]), F32)], axis=1
            ),
            jnp.zeros((10, share), F32),
        ],
        axis=0,
    )
    out[share:, :] = jnp.zeros((16, out.shape[1]), BF)
    out[share:, :share] = tail.astype(BF)


def ordered(f, parts):
    out = []
    for p in range(len(parts)):
        value = parts[0]
        for k in range(1, len(parts)):
            value = jnp.where(jnp.bitwise_xor(f, k) == p, parts[k], value)
        out.append(value)
    return out


def fill(f, blocks, w, first):
    share = w.shape[0] // len(blocks)
    for k, blk in enumerate(blocks):
        start = pl.multiple_of(jnp.bitwise_xor(f, k) * share, 16)
        w[pl.ds(start, share), first : first + blk.shape[1]] = blk[:share, :]


def front_kernel(nf, tile, f_ref, tok, cos, sin, qpos, kpos, *rest):
    blocks, kv_blocks, rest = rest[:nf], rest[nf : 2 * nf], rest[2 * nf :]
    normed_o, kraw_o, kv_o, qraw_o, q_o, att_o, low_o, tot_o, gains, hg, w = rest
    f = f_ref[0]
    share = w.shape[0] // nf
    rows = qpos.shape[0]
    proj = HEADS * HEAD_DIM
    scale = 1.0 / math.sqrt(HEAD_DIM)
    count = tok.shape[0] // tile
    fill(f, blocks, w, 0)
    fill(f, kv_blocks, w, proj)
    extra = ordered(f, [b[share:, :].astype(F32) for b in kv_blocks])
    gains[...] = jnp.concatenate([e[:4, :share] for e in extra], axis=1)
    hg[...] = jnp.concatenate([e[4:6, : HEAD_DIM // nf] for e in extra], axis=1)
    bound = bound_of(hg)

    def keys(t):
        part = tile_rows(t, tile, count)
        u, _ = unit(tok[part, :].astype(F32))
        normed = (u * gains[0:1, :]).astype(BF)
        normed_o[part, :] = normed
        out = dot(normed, w[:, proj:])
        key = out[:, :HEAD_DIM]
        kraw_o[part, :] = key
        u, _ = unit(key)
        kv_o[part, :HEAD_DIM] = rotate(u * hg[1:2, :], cos[part, :], sin[part, :]).astype(BF)
        kv_o[part, HEAD_DIM:] = out[:, HEAD_DIM:].astype(BF)

    tile_loop(count, keys)
    for h in range(HEADS):
        raw = dot(normed_o[:rows, :], w[:, h * HEAD_DIM : (h + 1) * HEAD_DIM])
        k = jnp.bitwise_xor(f, h)
        qraw_o[k] = raw
        u, _ = unit(raw)
        q_o[k] = rotate(u * hg[0:1, :], cos[:rows, :], sin[:rows, :]).astype(BF)
    for k in range(HEADS):

        def step(t, k=k):
            part = tile_rows(t, tile, count)
            raw = dot_nt(q_o[k], kv_o[part, :HEAD_DIM])
            allowed = kpos[:, part] <= qpos[...]
            terms = jnp.where(allowed, jnp.exp(raw * scale - bound), 0.0)
            total = jnp.sum(terms, axis=1, keepdims=True)
            num = dot(terms.astype(BF), kv_o[part, HEAD_DIM:])
            if count == 1:
                tot_o[k], att_o[k] = total, num
            else:
                tot_o[k] += total
                att_o[k] += num

        if count > 1:
            tot_o[k] = jnp.zeros_like(tot_o[k])
            att_o[k] = jnp.zeros_like(att_o[k])
        tile_loop(count, step)
        att = att_o[k] / tot_o[k]
        att_o[k] = att
        low_o[k] = att.astype(BF)


def mid_kernel(nf, tok, gains, att, *rest):
    wo = rest[:nf]
    branch_o, middle_o, ff_o = rest[nf:]
    branch = None
    for k in range(nf):
        term = dot(att[k], wo[k][...])
        branch = term if branch is None else branch + term
    branch_o[...] = branch
    u, _ = unit(branch)
    middle = tok[...].astype(F32) + u * gains[1:2, :]
    middle_o[...] = middle
    u, _ = unit(middle)
    ff_o[...] = (u * gains[2:3, :]).astype(BF)


def gelu_parts(v):
    t = jnp.tanh(0.7978845608028654 * (v + 0.044715 * v * v * v))
    half = 0.5 * (1.0 + t)
    slope = half + 0.5 * v * (1.0 - t * t) * 0.7978845608028654 * (1.0 + 3 * 0.044715 * v * v)
    return v * half, slope


def ff_kernel(mine, other, wg0, wu0, wd0, wg1, wu1, wd1, own_o, send_o, pack_o, hid_o, a_o, b_o):
    rows, d = mine.shape
    pack_o[:rows, :d] = mine[...]
    pack_o[rows:, :d] = other[...]
    x = pack_o[:, :d]
    mixed = None
    for i, (wg, wu, wd) in enumerate(((wg0, wu0, wd0), (wg1, wu1, wd1))):
        gate = dot(x, wg[...])
        up = dot(x, wu[...])
        value, slope = gelu_parts(gate)
        a_o[i] = value
        b_o[i] = up * slope
        hidden = (value * up).astype(BF)
        if i == 0:
            hid_o[...] = hidden
        else:
            pack_o[:, d:] = hidden
        term = dot(hidden, wd[...])
        mixed = term if mixed is None else mixed + term
    own_o[...] = mixed[:rows, :]
    send_o[...] = mixed[rows:, :].astype(BF)


def finish_kernel(own, got, middle, cot, gains, out_o, low_o, gain_o):
    u, r = unit(own[...] + got[...].astype(F32))
    out_o[...] = (middle[...] + u * gains[3:4, :]).astype(BF)
    grad, gain = norm_back(cot[...].astype(F32), u, r, gains[3:4, :])
    low_o[...] = grad.astype(BF)
    gain_o[...] = gain


def ff_back_kernel(
    mine, other, a, b, wg0, wu0, wd0, wg1, wu1, wd1, own_o, send_o, pack_o, gg_o
):
    rows, d = mine.shape
    width = wg0.shape[1]
    pack_o[:rows, :d] = mine[...]
    pack_o[rows:, :d] = other[...]
    c = pack_o[:, :d]
    total = None
    for i, (wg, wu, wd) in enumerate(((wg0, wu0, wd0), (wg1, wu1, wd1))):
        gh = dot_nt(c, wd[...])
        gg = (gh * b[i]).astype(BF)
        gu = (gh * a[i]).astype(BF)
        if i == 0:
            gg_o[:, :width] = gg
            gg_o[:, width:] = gu
        else:
            pack_o[:, d : d + width] = gg
            pack_o[:, d + width :] = gu
        term = dot_nt(gg, wg[...]) + dot_nt(gu, wu[...])
        total = term if total is None else total + term
    own_o[...] = total[:rows, :]
    send_o[...] = total[rows:, :].astype(BF)


def fold(out, at, grad, wide):
    rows = grad.shape[0]
    out[at : at + rows, :] = grad[:, :wide].astype(BF)
    strip = rows // 4
    parts = [grad[i * strip : (i + 1) * strip, wide:] for i in range(4)]
    out[at + rows : at + rows + strip, :] = jnp.concatenate(parts, axis=1).astype(BF)


def unfold(full, at, out):
    rows, wide = out.shape[0], full.shape[1]
    out[:, :wide] = full[at : at + rows]
    strip, piece = rows // 4, wide // 4
    for i in range(4):
        out[i * strip : (i + 1) * strip, wide:] = full[
            at + rows : at + rows + strip, i * piece : (i + 1) * piece
        ]


def ff_grad_kernel(pack1, hid, got1, pack2, gg, got2, gate_o, up_o, x_s, h_s, c_s, g_s):
    rows, width = hid.shape
    d = x_s.shape[1]
    x_s[:rows, :] = pack1[:, :d]
    x_s[rows:, :] = got1[:, :d]
    h_s[:rows, :] = hid[...]
    h_s[rows:, :] = got1[:, d:]
    c_s[:rows, :] = pack2[:, :d]
    c_s[rows:, :] = got2[:, :d]
    g_s[:rows, :] = gg[...]
    g_s[rows:, :] = got2[:, d:]
    gate_o[:d, :] = dot_tn(x_s[...], g_s[:, :width]).astype(BF)
    up_o[...] = dot_tn(x_s[...], g_s[:, width:]).astype(BF)
    fold(gate_o, d, dot_tn(h_s[...], c_s[...]), width)


def post_kernel(own, got, middle, branch, cot, gains, gbl_o, resid_o, gain_o):
    um, rm = unit(middle[...])
    grad, gain2 = norm_back(own[...] + got[...].astype(F32), um, rm, gains[2:3, :])
    grad_middle = cot[...].astype(F32) + grad
    resid_o[...] = grad_middle
    ub, rb = unit(branch[...])
    grad_branch, gain1 = norm_back(grad_middle, ub, rb, gains[1:2, :])
    gbl_o[...] = grad_branch.astype(BF)
    gain_o[...] = jnp.concatenate([gain1, gain2], axis=0)


def back_kernel(
    nf, tile, f_ref, gbl, gain12, gain3, att, tot, q, qraw, kv, normed, kraw, hg, cos, sin, qpos,
    kpos, *rest,
):
    wo = rest[:nf]
    far_o, own_o, next_o, odd_o, even_o, sg_s, tg_s, acc, s_s, e_s, kvw_s, gq_s = rest[nf:]
    f = f_ref[0]
    scale = 1.0 / math.sqrt(HEAD_DIM)
    rows, d = gbl.shape
    bound = bound_of(hg)
    count = kv.shape[0] // tile
    for k in range(HEADS):
        ga = dot_nt(gbl[...], wo[k][...])
        inv = 1.0 / tot[k]
        sg_s[k * rows : (k + 1) * rows, :] = (ga * inv).astype(BF)
        tg_s[k] = -jnp.sum(ga * att[k], axis=1, keepdims=True) * inv

    def step(t):
        part = tile_rows(t, tile, count)
        allowed = kpos[:, part] <= qpos[...]
        for k in range(HEADS):
            mine = slice(k * rows, (k + 1) * rows)
            raw = dot_nt(q[k], kv[part, :HEAD_DIM])
            terms = jnp.where(allowed, jnp.exp(raw * scale - bound), 0.0)
            e_s[mine, :] = terms.astype(BF)
            gp = dot_nt(sg_s[mine, :], kv[part, HEAD_DIM:])
            s = (terms * (gp + tg_s[k]) * scale).astype(BF)
            s_s[mine, :] = s
            term = dot(s, kv[part, :HEAD_DIM])
            if count == 1:
                acc[k] = term
            else:
                acc[k] += term
        queries = q[...].reshape(HEADS * rows, HEAD_DIM)
        c = rotate_back(dot_tn(s_s[...], queries), cos[part, :], sin[part, :])
        u, r = unit(kraw[part, :])
        gk, gain = norm_back(c, u, r, hg[1:2, :])
        gkl = gk.astype(BF)
        gvl = dot_tn(e_s[...], sg_s[...]).astype(BF)
        kk = dot_tn(normed[part, :], gkl)
        vv = dot_tn(normed[part, :], gvl)
        if count == 1:
            kvw_s[:d, :HEAD_DIM] = kk
            kvw_s[:d, HEAD_DIM:] = vv
            kvw_s[d : d + 1, :HEAD_DIM] = gain
        else:
            kvw_s[:d, :HEAD_DIM] += kk
            kvw_s[:d, HEAD_DIM:] += vv
            kvw_s[d : d + 1, :HEAD_DIM] += gain
        for j in range(tile // rows):
            out = even_o if j % 2 == 0 else odd_o
            start = (j // 2) * rows
            if count > 1:
                start = pl.multiple_of(t * (tile // 2) + start, rows)
            out[pl.ds(start, rows), :HEAD_DIM] = gkl[j * rows : (j + 1) * rows, :]
            out[pl.ds(start, rows), HEAD_DIM:] = gvl[j * rows : (j + 1) * rows, :]

    if count > 1:
        acc[...] = jnp.zeros_like(acc)
        kvw_s[...] = jnp.zeros_like(kvw_s)
    tile_loop(count, step)
    share = own_o.shape[0]
    lines = 2 * rows + 16
    for k, out in enumerate((own_o, next_o, None, None)):
        start = pl.multiple_of(jnp.bitwise_xor(f, k) * share, 16)
        chunk = kvw_s[pl.ds(start, share), :]
        if out is not None:
            out[...] = chunk
        else:
            at = lines + (k - 2) * share
            far_o[at : at + share, :] = chunk.astype(BF)
    gain = None
    for k in range(HEADS):
        u, r = unit(qraw[k])
        c = rotate_back(acc[k], cos[:rows, :], sin[:rows, :])
        grad, g = norm_back(c, u, r, hg[0:1, :])
        gain = g if gain is None else gain + g
        h = jnp.bitwise_xor(f, k)
        gq_s[:, pl.ds(pl.multiple_of(h * HEAD_DIM, HEAD_DIM), HEAD_DIM)] = grad.astype(BF)
    wide = 2 * HEAD_DIM
    far_o[:rows, :] = gq_s[:, :wide]
    far_o[rows : 2 * rows, :] = gq_s[:, wide:]
    three = jnp.concatenate([gain12[...], gain3[...]], axis=0)
    tail = jnp.concatenate(
        [three[i : i + 1, wide:] for i in range(3)] + [jnp.zeros((1, 4 * wide - 3 * d), F32)],
        axis=1,
    )
    heads = jnp.concatenate([gain, kvw_s[d : d + 1, :HEAD_DIM]], axis=1)
    pad = jnp.zeros((11, wide), F32)
    far_o[2 * rows : lines, :] = jnp.concatenate(
        [three[:, :wide], tail, heads, pad], axis=0
    ).astype(BF)


def relay_kernel(lines, mine, far, own, nxt, out_o, own_o):
    share = own.shape[0]
    out_o[:lines, :] = mine[:lines, :]
    out_o[lines : 2 * lines, :] = far[:lines, :]
    out_o[2 * lines :, :] = (nxt[...] + far[lines + share :, :].astype(F32)).astype(BF)
    own_o[...] = own[...] + far[lines : lines + share, :].astype(F32)


def query_grad_kernel(lines, mine, far, got, own, *rest):
    cols, (out_o, g_s, n_s) = rest[:4], rest[4:]
    rows, share = cols[0].shape[0], n_s.shape[1]
    wide = mine.shape[1]
    gain = None
    for k, (ref, at) in enumerate(((mine, 0), (got, 0), (far, 0), (got, lines))):
        mine_rows = slice(k * rows, (k + 1) * rows)
        g_s[mine_rows, :wide] = ref[at : at + rows, :]
        g_s[mine_rows, wide:] = ref[at + rows : at + 2 * rows, :]
        n_s[mine_rows, :] = cols[k][:, cols[k].shape[1] - share :]
        part = ref[at + 2 * rows : at + lines, :].astype(F32)
        gain = part if gain is None else gain + part
    qw = dot_tn(n_s[...], g_s[...])
    out_o[:share, :] = qw[:, :wide].astype(BF)
    out_o[share : 2 * share, :] = qw[:, wide:].astype(BF)
    out_o[2 * share : 3 * share, :] = (own[...] + got[2 * lines :, :].astype(F32)).astype(BF)
    out_o[3 * share : 3 * share + 16, :] = gain.astype(BF)
    out_o[3 * share + 16 :, :] = jnp.zeros((out_o.shape[0] - 3 * share - 16, wide), BF)


def out_grad_kernel(nf, up, *refs):
    cols, gbl, (out_o, a_s, b_s) = refs[:nf], refs[nf : 2 * nf], refs[2 * nf :]
    rows = gbl[0].shape[0]
    for k in range(nf):
        a_s[k * rows : (k + 1) * rows, :] = cols[k][:, : a_s.shape[1]]
        b_s[k * rows : (k + 1) * rows, :] = gbl[k][...]
    out_o[: up.shape[0], :] = up[...]
    fold(out_o, up.shape[0], dot_tn(a_s[...], b_s[...]), up.shape[1])


def joined(upper, mine, got):
    a, b = mine[...].astype(F32), got[...].astype(F32)
    return jnp.concatenate([jnp.where(upper, b, a), jnp.where(upper, a, b)], axis=0)


def last_ff_kernel(upper_ref, mine, got, first_o, second_o):
    full = joined(upper_ref[0] != 0, mine, got)
    rows = first_o.shape[0]
    first_o[...] = full[:rows]
    unfold(full, rows, second_o)


def last_kernel(upper_ref, mine, got, wq, wk, wv, q_o, k_o, v_o, p_o, rest_o):
    share = wq.shape[0]
    full = joined(upper_ref[0] != 0, mine, got)
    wide = full.shape[1]
    q_o[:, :wide] = full[:share]
    q_o[:, wide:] = full[share : 2 * share]
    k_o[...] = full[2 * share : 3 * share, :HEAD_DIM]
    v_o[...] = full[2 * share : 3 * share, HEAD_DIM:]
    total = jnp.sum(q_o[...] * wq[...].astype(F32), axis=1, keepdims=True)
    total += jnp.sum(k_o[...] * wk[...].astype(F32), axis=1, keepdims=True)
    p_o[...] = total + jnp.sum(v_o[...] * wv[...].astype(F32), axis=1, keepdims=True)
    rest_o[...] = full[3 * share : 3 * share + 16]


def input_back_kernel(nf, f_ref, tok, gkv, gq, resid, gains, *rest):
    blocks, kv_blocks, (grad_o, w) = rest[:nf], rest[nf : 2 * nf], rest[2 * nf :]
    rows = tok.shape[0]
    proj = HEADS * HEAD_DIM
    fill(f_ref[0], blocks, w, 0)
    fill(f_ref[0], kv_blocks, w, proj)
    low = gkv[...].astype(BF)
    wide = 2 * HEAD_DIM
    gn = dot_nt(gq[:rows, :], w[:, :wide]) + dot_nt(gq[rows : 2 * rows, :], w[:, wide:proj])
    gn = gn + dot_nt(low, w[:, proj:])
    u, r = unit(tok[...].astype(F32))
    gx, _ = norm_back(gn, u, r, gains[0:1, :])
    grad_o[...] = resid[...] + gx


def swap(x, axis, n, bit):
    return lax.ppermute(x, axis, [(i, i ^ bit) for i in range(n)])


class Order:
    def __init__(self):
        self.last = ()

    def arrived(self, *xs):
        out = lax.optimization_barrier(tuple(xs) + self.last)[: len(xs)]
        return out if len(xs) > 1 else out[0]

    def leaves(self, x):
        self.last = (x,)
        return x


def follow(x, *earlier):
    return lax.optimization_barrier((x,) + earlier)[0]


def gather_fsdp(x, n, *earlier):
    far = swap(x, "fsdp", n, 2)
    both = swap(jnp.concatenate([x, follow(far, *earlier)], axis=0), "fsdp", n, 1)
    rows = x.shape[0]
    return [x, both[:rows], far, both[rows:]]


def exchange_fsdp(blocks, n):
    return [b if k == 0 else swap(b, "fsdp", n, k) for k, b in enumerate(blocks)]


def gather_ctx(x, n):
    if n > 8:
        bit = 1
        while bit < n:
            x = jnp.concatenate([x, swap(x, "ctx", n, bit)], axis=0)
            bit *= 2
        return x, x
    far = {k: swap(x, "ctx", n, k) for k in range(n - 2, 0, -2)}
    near = swap(x, "ctx", n, 1)
    rows = x.shape[0]
    first = swap(far[2], "ctx", n, 1)
    ahead = jnp.concatenate([far[k] for k in range(4, n, 2)], axis=0)
    second = swap(ahead, "ctx", n, 1)
    parts = [x, near, far[2], first]
    for i, k in enumerate(range(4, n, 2)):
        parts += [far[k], second[i * rows : (i + 1) * rows]]
    return jnp.concatenate(parts, axis=0), ahead


def scatter_steps(odd, even, n, order, result):
    got = swap(order.leaves(odd), "ctx", n, 1)
    yield
    x = even.astype(F32) + order.arrived(got).astype(F32)
    rows = x.shape[0] * 2 // n
    if n > 8:
        bit = n // 2
        while bit > 1:
            half = x.shape[0] // 2
            got = swap(order.leaves(x[half:].astype(BF)), "ctx", n, bit)
            yield
            x = x[:half] + order.arrived(got).astype(F32)
            bit //= 2
        result.append(x)
        return
    low = order.leaves(x.astype(BF))
    got = [swap(low[k * rows : (k + 1) * rows], "ctx", n, 2 * k) for k in range(n // 2 - 1, 0, -1)]
    yield
    total = x[:rows]
    for g in order.arrived(*got):
        total = total + g.astype(F32)
    result.append(total)


def sum_steps(x, n, c, bits, order, result):
    for bit in bits:
        half = x.shape[0] // 2
        upper = (c & bit) != 0
        keep = jnp.where(upper, x[half:], x[:half])
        send = jnp.where(upper, x[:half], x[half:])
        got = swap(order.leaves(send), "ctx", n, bit)
        yield
        x = (keep.astype(F32) + order.arrived(got).astype(F32)).astype(BF)
    for bit in bits[:0:-1]:
        upper = (c & bit) != 0
        got = swap(order.leaves(x), "ctx", n, bit)
        yield
        got = order.arrived(got)
        x = jnp.concatenate([jnp.where(upper, got, x), jnp.where(upper, x, got)], axis=0)
    got = swap(order.leaves(x), "ctx", n, bits[0])
    yield
    result += [x, order.arrived(got)]


def short_sum_steps(x, n, c, order, result):
    half = x.shape[0] // 2
    upper = (c & 1) != 0
    keep = jnp.where(upper, x[half:], x[:half])
    send = jnp.where(upper, x[:half], x[half:])
    got = swap(order.leaves(send), "ctx", n, 1)
    yield
    x = keep.astype(F32) + order.arrived(got).astype(F32)
    count = n // 2
    rows = half // count
    z = c >> 1
    low = order.leaves(x.astype(BF))
    total = lax.dynamic_slice_in_dim(x, z * rows, rows, 0)
    got = []
    for j in range(count - 1, 0, -1):
        piece = lax.dynamic_slice_in_dim(low, (z ^ j) * rows, rows, 0)
        got.append(swap(piece, "ctx", n, 2 * j))
    yield
    for g in order.arrived(*got):
        total = total + g.astype(F32)
    mine = order.leaves(total.astype(BF))
    parts = [mine] + [swap(mine, "ctx", n, 2 * j) for j in range(1, count)]
    yield
    parts = order.arrived(*parts)
    x = jnp.zeros((half, x.shape[1]), BF)
    for j, p in enumerate(parts):
        x = lax.dynamic_update_slice_in_dim(x, p, (z ^ j) * rows, 0)
    got = swap(order.leaves(x), "ctx", n, 1)
    yield
    result += [x, order.arrived(got)]


def layer(
    nf,
    nc,
    tokens,
    cotangent,
    block_order,
    query_weight,
    key_weight,
    value_weight,
    out_weight,
    gate_weight,
    up_weight,
    down_weight,
    norm_gains,
    head_gains,
):
    rows, d = tokens.shape
    block_len = rows // 2
    f = lax.axis_index("fsdp")
    c = lax.axis_index("ctx")
    f_arr = f.reshape(1).astype(jnp.int32)
    seq = nc * rows
    tile = min(seq, 1024)
    proj = HEADS * HEAD_DIM
    width = gate_weight.shape[1]
    share = d // nf
    qkv = proj + 2 * HEAD_DIM
    hd = (HEADS, rows, HEAD_DIM)

    wq_far = swap(query_weight, "fsdp", nf, 2)
    tok_all, ahead = gather_ctx(tokens, nc)
    (kvpack,) = call(
        pack_kernel, [((share + 16, 2 * HEAD_DIM), BF)],
        key_weight, value_weight, norm_gains, head_gains,
    )

    slots = jnp.take(block_order.reshape(nc, 2), c ^ jnp.arange(nc), axis=0)
    pos = (slots.reshape(-1, 1) * block_len + jnp.arange(block_len)[None, :]).reshape(seq)
    kpos = pos.reshape(1, seq)
    qpos = pos[:rows].reshape(rows, 1)
    inv_freq = ROPE_BASE ** (-2.0 * jnp.arange(HEAD_DIM // 2, dtype=F32) / HEAD_DIM)
    angles = pos.astype(F32)[:, None] * inv_freq[None, :]
    cos, sin = jnp.cos(angles), jnp.sin(angles)

    wkv = gather_fsdp(kvpack, nf, ahead, cos, sin)
    both = swap(jnp.concatenate([query_weight, follow(wq_far, ahead)], axis=0), "fsdp", nf, 1)
    wq = [query_weight, both[:share], wq_far, both[share:]]
    wo = gather_fsdp(out_weight, nf, both, wkv[1])
    own_ff = (gate_weight, up_weight, down_weight)
    next_ff = [swap(w, "fsdp", nf, 1) for w in lax.optimization_barrier(own_ff + (wo[1],))[:3]]

    big = 36 if seq <= 1024 else 60
    normed, kraw, kv, qraw, q, att, att_low, tot, gains, hg = call(
        functools.partial(front_kernel, nf, tile),
        [
            ((seq, d), BF), ((seq, HEAD_DIM), F32), ((seq, 2 * HEAD_DIM), BF),
            (hd, F32), (hd, BF), (hd, F32), (hd, BF), ((HEADS, rows, 1), F32),
            ((4, d), F32), ((2, HEAD_DIM), F32),
        ],
        f_arr, tok_all, cos, sin, qpos, kpos, *wq, *wkv,
        scratch=[pltpu.VMEM((d, qkv), BF)], smem=1, vmem=big, us=6,
    )
    branch, middle, ff_in = call(
        functools.partial(mid_kernel, nf),
        [((rows, d), F32), ((rows, d), F32), ((rows, d), BF)],
        tokens, gains, att_low, *wo, us=0.6,
    )
    cols = exchange_fsdp(
        [
            jnp.concatenate(
                [att_low[k], lax.dynamic_slice_in_dim(normed[:rows], (f ^ k) * share, share, 1)],
                axis=1,
            )
            for k in range(nf)
        ],
        nf,
    )
    two = 2 * rows
    own, send, pack1, hid, act, slope = call(
        ff_kernel,
        [
            ((rows, d), F32), ((rows, d), BF), ((two, d + width), BF), ((two, width), BF),
            ((2, two, width), F32), ((2, two, width), F32),
        ],
        ff_in, swap(ff_in, "fsdp", nf, 2), *own_ff, *next_ff, us=3.6,
    )
    got1 = swap(pack1, "fsdp", nf, 1)
    output, gml, gain3 = call(
        finish_kernel,
        [((rows, d), BF), ((rows, d), BF), ((1, d), F32)],
        own, swap(send, "fsdp", nf, 2), middle, cotangent, gains, after=cols[1:],
    )
    own, send, pack2, gg = call(
        ff_back_kernel,
        [((rows, d), F32), ((rows, d), BF), ((two, d + 2 * width), BF), ((two, 2 * width), BF)],
        gml, swap(gml, "fsdp", nf, 2), act, slope, *own_ff, *next_ff,
        us=3.6, after=[got1],
    )
    got2 = swap(pack2, "fsdp", nf, 1)
    got = swap(send, "fsdp", nf, 2)
    p_part, up_part = call(
        ff_grad_kernel,
        [((d + width + width // 4, width), BF), ((d, width), BF)],
        pack1, hid, got1, pack2, gg, got2,
        scratch=[
            pltpu.VMEM((2 * two, d), BF),
            pltpu.VMEM((2 * two, width), BF),
            pltpu.VMEM((2 * two, d), BF),
            pltpu.VMEM((2 * two, 2 * width), BF),
        ],
        us=2.5,
    )
    order = Order()
    up_bits = [1 << i for i in range(nc.bit_length() - 1)]
    alt_bits = up_bits[1:2] + up_bits[:1] + up_bits[2:]
    p_sum, q_sum, a_sum, kv_sum = [], [], [], []
    p_steps = sum_steps(p_part, nc, c, up_bits, order, p_sum)
    next(p_steps)
    gbl, resid, gain12 = call(
        post_kernel,
        [((rows, d), BF), ((rows, d), F32), ((2, d), F32)],
        own, got, middle, branch, cotangent, gains, after=order.last,
    )
    gbl_far = swap(gbl, "fsdp", nf, 2)
    lines = 2 * rows + 16
    wide = 2 * HEAD_DIM
    ybuf, kvw0, kvw1, odd, even = call(
        functools.partial(back_kernel, nf, tile),
        [
            ((lines + 2 * share, wide), BF),
            ((share, wide), F32),
            ((share, wide), F32),
            ((seq // 2, wide), BF),
            ((seq // 2, wide), BF),
        ],
        f_arr, gbl, gain12, gain3, att, tot, q, qraw, kv, normed, kraw, hg, cos, sin, qpos, kpos,
        *wo,
        scratch=[
            pltpu.VMEM((HEADS * rows, HEAD_DIM), BF),
            pltpu.VMEM((HEADS, rows, 1), F32),
            pltpu.VMEM(hd, F32),
            pltpu.VMEM((HEADS * rows, tile), BF),
            pltpu.VMEM((HEADS * rows, tile), BF),
            pltpu.VMEM((d + 8, wide), F32),
            pltpu.VMEM((rows, proj), BF),
        ],
        smem=1, vmem=big, us=9,
    )
    far = swap(order.leaves(ybuf), "fsdp", nf, 2)
    gbl_both = swap(
        order.leaves(jnp.concatenate([gbl, order.arrived(gbl_far)], axis=0)), "fsdp", nf, 1
    )
    next(p_steps)
    gbl_both = order.arrived(gbl_both)
    (q_part,) = call(
        functools.partial(out_grad_kernel, nf),
        [((d + (proj // nf) * 5 // 4, width), BF)],
        up_part, *cols, gbl, gbl_both[:rows], gbl_far, gbl_both[rows:],
        scratch=[pltpu.VMEM((nf * rows, proj // nf), BF), pltpu.VMEM((nf * rows, d), BF)],
        us=1.3,
    )
    q_steps = sum_steps(q_part, nc, c, alt_bits, order, q_sum)
    next(q_steps)
    kv_steps = scatter_steps(odd, even, nc, order, kv_sum)
    next(kv_steps)

    far = order.arrived(far)
    cbuf, kvw = call(
        functools.partial(relay_kernel, lines),
        [((2 * lines + share, wide), BF), ((share, wide), F32)],
        ybuf, far, kvw0, kvw1,
    )
    near = swap(order.leaves(cbuf), "fsdp", nf, 1)
    next(p_steps)
    near = order.arrived(near)
    (att_part,) = call(
        functools.partial(query_grad_kernel, lines),
        [((-(-(3 * share + 16) // 128) * 128, wide), BF)],
        ybuf, far, near, kvw, *cols,
        scratch=[pltpu.VMEM((nf * rows, proj), BF), pltpu.VMEM((nf * rows, share), BF)],
    )
    if nc > 8:
        a_steps = sum_steps(att_part, nc, c, up_bits, order, a_sum)
    else:
        a_steps = short_sum_steps(att_part, nc, c, order, a_sum)
    next(a_steps)
    turns = [q_steps, kv_steps, p_steps, a_steps, q_steps, kv_steps, p_steps, a_steps, q_steps]
    turns += [p_steps, a_steps, q_steps, a_steps, q_steps, p_steps]
    for steps in turns:
        next(steps, None)
    for steps in (a_steps, q_steps, p_steps, kv_steps):
        for _ in steps:
            pass

    (input_grad,) = call(
        functools.partial(input_back_kernel, nf),
        [((rows, d), F32)],
        f_arr, tokens, kv_sum[0], ybuf, resid, gains, *wq, *wkv,
        scratch=[pltpu.VMEM((d, qkv), BF)], smem=1, us=1.7,
    )
    upper = (c & up_bits[0]).reshape(1).astype(jnp.int32)
    grad_gate, grad_down = call(
        last_ff_kernel, [((d, width), F32), ((width, d), F32)], upper, *p_sum, smem=1
    )
    grad_up, grad_out = call(
        last_ff_kernel, [((d, width), F32), ((proj // nf, d), F32)],
        (c & alt_bits[0]).reshape(1).astype(jnp.int32), *q_sum, smem=1,
    )
    grad_q, grad_k, grad_v, gain0, gain_sum = call(
        last_kernel,
        [
            ((share, proj), F32), ((share, HEAD_DIM), F32), ((share, HEAD_DIM), F32),
            ((share, 1), F32), ((16, wide), F32),
        ],
        upper, *a_sum, query_weight, key_weight, value_weight, smem=1,
    )
    gain0 = gain0.reshape(1, share) / norm_gains[0:1].astype(F32)
    rest = gain_sum[3, : 3 * (d - wide)].reshape(3, d - wide)
    others = jnp.concatenate([gain_sum[:3], rest], axis=1)
    others = lax.dynamic_slice_in_dim(others, f * share, share, 1)
    heads = gain_sum[4].reshape(2, HEAD_DIM)
    return (
        output,
        input_grad,
        grad_q,
        grad_k,
        grad_v,
        grad_out,
        grad_gate,
        grad_up,
        grad_down,
        jnp.concatenate([gain0, others], axis=0),
        lax.dynamic_slice_in_dim(heads, f * (HEAD_DIM // nf), HEAD_DIM // nf, 1),
    )


def solution(mesh):
    row = P(("ctx", "fsdp"), None)
    first, second = P("fsdp", None), P(None, "fsdp")
    body = functools.partial(layer, mesh.shape["fsdp"], mesh.shape["ctx"])
    return jax.shard_map(
        body,
        mesh=mesh,
        in_specs=(row, row, P(), first, first, first, first, second, second, first, second, second),
        out_specs=(row, row, first, first, first, first, second, second, first, second, second),
        check_vma=False,
    )
```

```python
import functools
import math

import jax
import jax.numpy as jnp
from jax import lax
from jax.experimental import pallas as pl
from jax.experimental.pallas import tpu as pltpu
from jax.sharding import PartitionSpec as P

HEADS = 4
HEAD_DIM = 256
NORM_EPS = 1e-06
ROPE_BASE = 1000000.0
BF = jnp.bfloat16
F32 = jnp.float32
MIB = 1024 * 1024


def dot(a, b):
    return lax.dot_general(a, b, (((1,), (0,)), ((), ())), preferred_element_type=F32)


def dot_nt(a, b):
    return lax.dot_general(a, b, (((1,), (1,)), ((), ())), preferred_element_type=F32)


def dot_tn(a, b):
    return lax.dot_general(a, b, (((0,), (0,)), ((), ())), preferred_element_type=F32)


def unit(v):
    r = lax.rsqrt(jnp.mean(v * v, axis=-1, keepdims=True) + NORM_EPS)
    return v * r, r


def norm_back(c, u, r, g):
    cg = c * g
    grad = r * (cg - u * jnp.mean(cg * u, axis=-1, keepdims=True))
    return grad, jnp.sum(c * u, axis=0, keepdims=True)


def rotate(v, cos, sin):
    half = v.shape[-1] // 2
    a, b = v[:, :half], v[:, half:]
    return jnp.concatenate([a * cos - b * sin, b * cos + a * sin], axis=-1)


def rotate_back(v, cos, sin):
    half = v.shape[-1] // 2
    a, b = v[:, :half], v[:, half:]
    return jnp.concatenate([a * cos + b * sin, b * cos - a * sin], axis=-1)


def call(kernel, outs, *args, scratch=(), vmem=16, us=1.0, smem=0, after=()):
    specs = [pl.BlockSpec(memory_space=pltpu.VMEM)] * len(args)
    for i in range(smem):
        specs[i] = pl.BlockSpec(memory_space=pltpu.SMEM)
    specs += [pl.BlockSpec(memory_space=pl.ANY)] * len(after)
    moved = sum(math.prod(a.shape) * a.dtype.itemsize for a in args)
    used, skip = len(args), len(args) + len(after)

    def body(*refs):
        kernel(*refs[:used], *refs[skip:])

    return pl.pallas_call(
        body,
        out_shape=[jax.ShapeDtypeStruct(s, d) for s, d in outs],
        in_specs=specs,
        out_specs=[pl.BlockSpec(memory_space=pltpu.VMEM)] * len(outs),
        scratch_shapes=list(scratch),
        compiler_params=pltpu.CompilerParams(vmem_limit_bytes=vmem * MIB),
        cost_estimate=pl.CostEstimate(
            flops=int(us * 1.1e9), bytes_accessed=moved, transcendentals=0
        ),
    )(*args, *after)


def bound_of(hg):
    peak = jnp.max(jnp.abs(hg[...]), axis=1, keepdims=True)
    return math.sqrt(HEAD_DIM) * peak[0:1, :] * peak[1:2, :]


def tile_loop(count, step):
    if count == 1:
        step(0)
    else:

        def body(t, carry):
            step(t)
            return carry

        lax.fori_loop(0, count, body, 0)


def tile_rows(t, tile, count):
    return pl.ds(pl.multiple_of(t * tile, tile), tile) if count > 1 else slice(None)


def pack_kernel(wk, wv, ng, hg, out):
    share = wk.shape[0]
    out[:share, :HEAD_DIM] = wk[...]
    out[:share, HEAD_DIM:] = wv[...]
    tail = jnp.concatenate(
        [
            ng[...].astype(F32),
            jnp.concatenate(
                [hg[...].astype(F32), jnp.zeros((2, share - hg.shape[1]), F32)], axis=1
            ),
            jnp.zeros((10, share), F32),
        ],
        axis=0,
    )
    out[share:, :] = jnp.zeros((16, out.shape[1]), BF)
    out[share:, :share] = tail.astype(BF)


def ordered(f, parts):
    out = []
    for p in range(len(parts)):
        value = parts[0]
        for k in range(1, len(parts)):
            value = jnp.where(jnp.bitwise_xor(f, k) == p, parts[k], value)
        out.append(value)
    return out


def fill(f, blocks, w, first):
    share = w.shape[0] // len(blocks)
    for k, blk in enumerate(blocks):
        start = pl.multiple_of(jnp.bitwise_xor(f, k) * share, 16)
        w[pl.ds(start, share), first : first + blk.shape[1]] = blk[:share, :]


def front_kernel(nf, tile, f_ref, tok, cos, sin, qpos, kpos, *rest):
    blocks, kv_blocks, rest = rest[:nf], rest[nf : 2 * nf], rest[2 * nf :]
    normed_o, kraw_o, kv_o, qraw_o, q_o, att_o, low_o, tot_o, gains, hg, w = rest
    f = f_ref[0]
    share = w.shape[0] // nf
    rows = qpos.shape[0]
    proj = HEADS * HEAD_DIM
    scale = 1.0 / math.sqrt(HEAD_DIM)
    count = tok.shape[0] // tile
    fill(f, blocks, w, 0)
    fill(f, kv_blocks, w, proj)
    extra = ordered(f, [b[share:, :].astype(F32) for b in kv_blocks])
    gains[...] = jnp.concatenate([e[:4, :share] for e in extra], axis=1)
    hg[...] = jnp.concatenate([e[4:6, : HEAD_DIM // nf] for e in extra], axis=1)
    bound = bound_of(hg)

    def keys(t):
        part = tile_rows(t, tile, count)
        u, _ = unit(tok[part, :].astype(F32))
        normed = (u * gains[0:1, :]).astype(BF)
        normed_o[part, :] = normed
        out = dot(normed, w[:, proj:])
        key = out[:, :HEAD_DIM]
        kraw_o[part, :] = key
        u, _ = unit(key)
        kv_o[part, :HEAD_DIM] = rotate(u * hg[1:2, :], cos[part, :], sin[part, :]).astype(BF)
        kv_o[part, HEAD_DIM:] = out[:, HEAD_DIM:].astype(BF)

    tile_loop(count, keys)
    for h in range(HEADS):
        raw = dot(normed_o[:rows, :], w[:, h * HEAD_DIM : (h + 1) * HEAD_DIM])
        k = jnp.bitwise_xor(f, h)
        qraw_o[k] = raw
        u, _ = unit(raw)
        q_o[k] = rotate(u * hg[0:1, :], cos[:rows, :], sin[:rows, :]).astype(BF)
    for k in range(HEADS):

        def step(t, k=k):
            part = tile_rows(t, tile, count)
            raw = dot_nt(q_o[k], kv_o[part, :HEAD_DIM])
            allowed = kpos[:, part] <= qpos[...]
            terms = jnp.where(allowed, jnp.exp(raw * scale - bound), 0.0)
            total = jnp.sum(terms, axis=1, keepdims=True)
            num = dot(terms.astype(BF), kv_o[part, HEAD_DIM:])
            if count == 1:
                tot_o[k], att_o[k] = total, num
            else:
                tot_o[k] += total
                att_o[k] += num

        if count > 1:
            tot_o[k] = jnp.zeros_like(tot_o[k])
            att_o[k] = jnp.zeros_like(att_o[k])
        tile_loop(count, step)
        att = att_o[k] / tot_o[k]
        att_o[k] = att
        low_o[k] = att.astype(BF)


def mid_kernel(nf, tok, gains, att, *rest):
    wo = rest[:nf]
    branch_o, middle_o, ff_o = rest[nf:]
    branch = None
    for k in range(nf):
        term = dot(att[k], wo[k][...])
        branch = term if branch is None else branch + term
    branch_o[...] = branch
    u, _ = unit(branch)
    middle = tok[...].astype(F32) + u * gains[1:2, :]
    middle_o[...] = middle
    u, _ = unit(middle)
    ff_o[...] = (u * gains[2:3, :]).astype(BF)


def gelu_parts(v):
    t = jnp.tanh(0.7978845608028654 * (v + 0.044715 * v * v * v))
    half = 0.5 * (1.0 + t)
    slope = half + 0.5 * v * (1.0 - t * t) * 0.7978845608028654 * (1.0 + 3 * 0.044715 * v * v)
    return v * half, slope


def ff_kernel(mine, other, wg0, wu0, wd0, wg1, wu1, wd1, own_o, send_o, pack_o, hid_o, a_o, b_o):
    rows, d = mine.shape
    pack_o[:rows, :d] = mine[...]
    pack_o[rows:, :d] = other[...]
    x = pack_o[:, :d]
    mixed = None
    for i, (wg, wu, wd) in enumerate(((wg0, wu0, wd0), (wg1, wu1, wd1))):
        gate = dot(x, wg[...])
        up = dot(x, wu[...])
        value, slope = gelu_parts(gate)
        a_o[i] = value
        b_o[i] = up * slope
        hidden = (value * up).astype(BF)
        if i == 0:
            hid_o[...] = hidden
        else:
            pack_o[:, d:] = hidden
        term = dot(hidden, wd[...])
        mixed = term if mixed is None else mixed + term
    own_o[...] = mixed[:rows, :]
    send_o[...] = mixed[rows:, :].astype(BF)


def finish_kernel(own, got, middle, cot, gains, out_o, low_o, gain_o):
    u, r = unit(own[...] + got[...].astype(F32))
    out_o[...] = (middle[...] + u * gains[3:4, :]).astype(BF)
    grad, gain = norm_back(cot[...].astype(F32), u, r, gains[3:4, :])
    low_o[...] = grad.astype(BF)
    gain_o[...] = gain


def ff_back_kernel(
    mine, other, a, b, wg0, wu0, wd0, wg1, wu1, wd1, own_o, send_o, pack_o, gg_o
):
    rows, d = mine.shape
    width = wg0.shape[1]
    pack_o[:rows, :d] = mine[...]
    pack_o[rows:, :d] = other[...]
    c = pack_o[:, :d]
    total = None
    for i, (wg, wu, wd) in enumerate(((wg0, wu0, wd0), (wg1, wu1, wd1))):
        gh = dot_nt(c, wd[...])
        gg = (gh * b[i]).astype(BF)
        gu = (gh * a[i]).astype(BF)
        if i == 0:
            gg_o[:, :width] = gg
            gg_o[:, width:] = gu
        else:
            pack_o[:, d : d + width] = gg
            pack_o[:, d + width :] = gu
        term = dot_nt(gg, wg[...]) + dot_nt(gu, wu[...])
        total = term if total is None else total + term
    own_o[...] = total[:rows, :]
    send_o[...] = total[rows:, :].astype(BF)


def fold(out, at, grad, wide):
    rows = grad.shape[0]
    out[at : at + rows, :] = grad[:, :wide].astype(BF)
    strip = rows // 4
    parts = [grad[i * strip : (i + 1) * strip, wide:] for i in range(4)]
    out[at + rows : at + rows + strip, :] = jnp.concatenate(parts, axis=1).astype(BF)


def unfold(full, at, out):
    rows, wide = out.shape[0], full.shape[1]
    out[:, :wide] = full[at : at + rows]
    strip, piece = rows // 4, wide // 4
    for i in range(4):
        out[i * strip : (i + 1) * strip, wide:] = full[
            at + rows : at + rows + strip, i * piece : (i + 1) * piece
        ]


def ff_grad_kernel(pack1, hid, got1, pack2, gg, got2, gate_o, up_o, x_s, h_s, c_s, g_s):
    rows, width = hid.shape
    d = x_s.shape[1]
    x_s[:rows, :] = pack1[:, :d]
    x_s[rows:, :] = got1[:, :d]
    h_s[:rows, :] = hid[...]
    h_s[rows:, :] = got1[:, d:]
    c_s[:rows, :] = pack2[:, :d]
    c_s[rows:, :] = got2[:, :d]
    g_s[:rows, :] = gg[...]
    g_s[rows:, :] = got2[:, d:]
    gate_o[:d, :] = dot_tn(x_s[...], g_s[:, :width]).astype(BF)
    up_o[...] = dot_tn(x_s[...], g_s[:, width:]).astype(BF)
    fold(gate_o, d, dot_tn(h_s[...], c_s[...]), width)


def post_kernel(own, got, middle, branch, cot, gains, gbl_o, resid_o, gain_o):
    um, rm = unit(middle[...])
    grad, gain2 = norm_back(own[...] + got[...].astype(F32), um, rm, gains[2:3, :])
    grad_middle = cot[...].astype(F32) + grad
    resid_o[...] = grad_middle
    ub, rb = unit(branch[...])
    grad_branch, gain1 = norm_back(grad_middle, ub, rb, gains[1:2, :])
    gbl_o[...] = grad_branch.astype(BF)
    gain_o[...] = jnp.concatenate([gain1, gain2], axis=0)


def back_kernel(
    nf, tile, f_ref, gbl, gain12, gain3, att, tot, q, qraw, kv, normed, kraw, hg, cos, sin, qpos,
    kpos, *rest,
):
    wo = rest[:nf]
    far_o, own_o, next_o, odd_o, even_o, sg_s, tg_s, acc, s_s, e_s, kvw_s, gq_s = rest[nf:]
    f = f_ref[0]
    scale = 1.0 / math.sqrt(HEAD_DIM)
    rows, d = gbl.shape
    bound = bound_of(hg)
    count = kv.shape[0] // tile
    for k in range(HEADS):
        ga = dot_nt(gbl[...], wo[k][...])
        inv = 1.0 / tot[k]
        sg_s[k * rows : (k + 1) * rows, :] = (ga * inv).astype(BF)
        tg_s[k] = -jnp.sum(ga * att[k], axis=1, keepdims=True) * inv

    def step(t):
        part = tile_rows(t, tile, count)
        allowed = kpos[:, part] <= qpos[...]
        for k in range(HEADS):
            mine = slice(k * rows, (k + 1) * rows)
            raw = dot_nt(q[k], kv[part, :HEAD_DIM])
            terms = jnp.where(allowed, jnp.exp(raw * scale - bound), 0.0)
            e_s[mine, :] = terms.astype(BF)
            gp = dot_nt(sg_s[mine, :], kv[part, HEAD_DIM:])
            s = (terms * (gp + tg_s[k]) * scale).astype(BF)
            s_s[mine, :] = s
            term = dot(s, kv[part, :HEAD_DIM])
            if count == 1:
                acc[k] = term
            else:
                acc[k] += term
        queries = q[...].reshape(HEADS * rows, HEAD_DIM)
        c = rotate_back(dot_tn(s_s[...], queries), cos[part, :], sin[part, :])
        u, r = unit(kraw[part, :])
        gk, gain = norm_back(c, u, r, hg[1:2, :])
        gkl = gk.astype(BF)
        gvl = dot_tn(e_s[...], sg_s[...]).astype(BF)
        kk = dot_tn(normed[part, :], gkl)
        vv = dot_tn(normed[part, :], gvl)
        if count == 1:
            kvw_s[:d, :HEAD_DIM] = kk
            kvw_s[:d, HEAD_DIM:] = vv
            kvw_s[d : d + 1, :HEAD_DIM] = gain
        else:
            kvw_s[:d, :HEAD_DIM] += kk
            kvw_s[:d, HEAD_DIM:] += vv
            kvw_s[d : d + 1, :HEAD_DIM] += gain
        for j in range(tile // rows):
            out = even_o if j % 2 == 0 else odd_o
            start = (j // 2) * rows
            if count > 1:
                start = pl.multiple_of(t * (tile // 2) + start, rows)
            out[pl.ds(start, rows), :HEAD_DIM] = gkl[j * rows : (j + 1) * rows, :]
            out[pl.ds(start, rows), HEAD_DIM:] = gvl[j * rows : (j + 1) * rows, :]

    if count > 1:
        acc[...] = jnp.zeros_like(acc)
        kvw_s[...] = jnp.zeros_like(kvw_s)
    tile_loop(count, step)
    share = own_o.shape[0]
    lines = 2 * rows + 16
    for k, out in enumerate((own_o, next_o, None, None)):
        start = pl.multiple_of(jnp.bitwise_xor(f, k) * share, 16)
        chunk = kvw_s[pl.ds(start, share), :]
        if out is not None:
            out[...] = chunk
        else:
            at = lines + (k - 2) * share
            far_o[at : at + share, :] = chunk.astype(BF)
    gain = None
    for k in range(HEADS):
        u, r = unit(qraw[k])
        c = rotate_back(acc[k], cos[:rows, :], sin[:rows, :])
        grad, g = norm_back(c, u, r, hg[0:1, :])
        gain = g if gain is None else gain + g
        h = jnp.bitwise_xor(f, k)
        gq_s[:, pl.ds(pl.multiple_of(h * HEAD_DIM, HEAD_DIM), HEAD_DIM)] = grad.astype(BF)
    wide = 2 * HEAD_DIM
    far_o[:rows, :] = gq_s[:, :wide]
    far_o[rows : 2 * rows, :] = gq_s[:, wide:]
    three = jnp.concatenate([gain12[...], gain3[...]], axis=0)
    tail = jnp.concatenate(
        [three[i : i + 1, wide:] for i in range(3)] + [jnp.zeros((1, 4 * wide - 3 * d), F32)],
        axis=1,
    )
    heads = jnp.concatenate([gain, kvw_s[d : d + 1, :HEAD_DIM]], axis=1)
    pad = jnp.zeros((11, wide), F32)
    far_o[2 * rows : lines, :] = jnp.concatenate(
        [three[:, :wide], tail, heads, pad], axis=0
    ).astype(BF)


def relay_kernel(lines, mine, far, own, nxt, out_o, own_o):
    share = own.shape[0]
    out_o[:lines, :] = mine[:lines, :]
    out_o[lines : 2 * lines, :] = far[:lines, :]
    out_o[2 * lines :, :] = (nxt[...] + far[lines + share :, :].astype(F32)).astype(BF)
    own_o[...] = own[...] + far[lines : lines + share, :].astype(F32)


def query_grad_kernel(lines, mine, far, got, own, *rest):
    cols, (out_o, g_s, n_s) = rest[:4], rest[4:]
    rows, share = cols[0].shape[0], n_s.shape[1]
    wide = mine.shape[1]
    gain = None
    for k, (ref, at) in enumerate(((mine, 0), (got, 0), (far, 0), (got, lines))):
        mine_rows = slice(k * rows, (k + 1) * rows)
        g_s[mine_rows, :wide] = ref[at : at + rows, :]
        g_s[mine_rows, wide:] = ref[at + rows : at + 2 * rows, :]
        n_s[mine_rows, :] = cols[k][:, cols[k].shape[1] - share :]
        part = ref[at + 2 * rows : at + lines, :].astype(F32)
        gain = part if gain is None else gain + part
    qw = dot_tn(n_s[...], g_s[...])
    out_o[:share, :] = qw[:, :wide].astype(BF)
    out_o[share : 2 * share, :] = qw[:, wide:].astype(BF)
    out_o[2 * share : 3 * share, :] = (own[...] + got[2 * lines :, :].astype(F32)).astype(BF)
    out_o[3 * share : 3 * share + 16, :] = gain.astype(BF)
    out_o[3 * share + 16 :, :] = jnp.zeros((out_o.shape[0] - 3 * share - 16, wide), BF)


def out_grad_kernel(nf, up, *refs):
    cols, gbl, (out_o, a_s, b_s) = refs[:nf], refs[nf : 2 * nf], refs[2 * nf :]
    rows = gbl[0].shape[0]
    for k in range(nf):
        a_s[k * rows : (k + 1) * rows, :] = cols[k][:, : a_s.shape[1]]
        b_s[k * rows : (k + 1) * rows, :] = gbl[k][...]
    out_o[: up.shape[0], :] = up[...]
    fold(out_o, up.shape[0], dot_tn(a_s[...], b_s[...]), up.shape[1])


def joined(upper, mine, got):
    a, b = mine[...].astype(F32), got[...].astype(F32)
    return jnp.concatenate([jnp.where(upper, b, a), jnp.where(upper, a, b)], axis=0)


def last_ff_kernel(upper_ref, mine, got, first_o, second_o):
    full = joined(upper_ref[0] != 0, mine, got)
    rows = first_o.shape[0]
    first_o[...] = full[:rows]
    unfold(full, rows, second_o)


def last_kernel(upper_ref, mine, got, wq, wk, wv, q_o, k_o, v_o, p_o, rest_o):
    share = wq.shape[0]
    full = joined(upper_ref[0] != 0, mine, got)
    wide = full.shape[1]
    q_o[:, :wide] = full[:share]
    q_o[:, wide:] = full[share : 2 * share]
    k_o[...] = full[2 * share : 3 * share, :HEAD_DIM]
    v_o[...] = full[2 * share : 3 * share, HEAD_DIM:]
    total = jnp.sum(q_o[...] * wq[...].astype(F32), axis=1, keepdims=True)
    total += jnp.sum(k_o[...] * wk[...].astype(F32), axis=1, keepdims=True)
    p_o[...] = total + jnp.sum(v_o[...] * wv[...].astype(F32), axis=1, keepdims=True)
    rest_o[...] = full[3 * share : 3 * share + 16]


def input_back_kernel(nf, f_ref, tok, gkv, gq, resid, gains, *rest):
    blocks, kv_blocks, (grad_o, w) = rest[:nf], rest[nf : 2 * nf], rest[2 * nf :]
    rows = tok.shape[0]
    proj = HEADS * HEAD_DIM
    fill(f_ref[0], blocks, w, 0)
    fill(f_ref[0], kv_blocks, w, proj)
    low = gkv[...].astype(BF)
    wide = 2 * HEAD_DIM
    gn = dot_nt(gq[:rows, :], w[:, :wide]) + dot_nt(gq[rows : 2 * rows, :], w[:, wide:proj])
    gn = gn + dot_nt(low, w[:, proj:])
    u, r = unit(tok[...].astype(F32))
    gx, _ = norm_back(gn, u, r, gains[0:1, :])
    grad_o[...] = resid[...] + gx


def swap(x, axis, n, bit):
    return lax.ppermute(x, axis, [(i, i ^ bit) for i in range(n)])


class Order:
    def __init__(self):
        self.last = ()

    def arrived(self, *xs):
        out = lax.optimization_barrier(tuple(xs) + self.last)[: len(xs)]
        return out if len(xs) > 1 else out[0]

    def leaves(self, x):
        self.last = (x,)
        return x


def follow(x, *earlier):
    return lax.optimization_barrier((x,) + earlier)[0]


def gather_fsdp(x, n, *earlier):
    far = swap(x, "fsdp", n, 2)
    both = swap(jnp.concatenate([x, follow(far, *earlier)], axis=0), "fsdp", n, 1)
    rows = x.shape[0]
    return [x, both[:rows], far, both[rows:]]


def exchange_fsdp(blocks, n):
    return [b if k == 0 else swap(b, "fsdp", n, k) for k, b in enumerate(blocks)]


def gather_ctx(x, n):
    if n > 8:
        bit = 1
        while bit < n:
            x = jnp.concatenate([x, swap(x, "ctx", n, bit)], axis=0)
            bit *= 2
        return x, x
    far = {k: swap(x, "ctx", n, k) for k in range(n - 2, 0, -2)}
    rows = x.shape[0]
    first = swap(jnp.concatenate([x, far[2]], axis=0), "ctx", n, 1)
    ahead = jnp.concatenate([far[k] for k in range(4, n, 2)], axis=0)
    second = swap(ahead, "ctx", n, 1)
    parts = [x, first[:rows], far[2], first[rows:]]
    for i, k in enumerate(range(4, n, 2)):
        parts += [far[k], second[i * rows : (i + 1) * rows]]
    return jnp.concatenate(parts, axis=0), ahead


def scatter_steps(odd, even, n, order, result):
    got = swap(order.leaves(odd), "ctx", n, 1)
    yield
    x = even.astype(F32) + order.arrived(got).astype(F32)
    rows = x.shape[0] * 2 // n
    if n > 8:
        bit = n // 2
        while bit > 1:
            half = x.shape[0] // 2
            got = swap(order.leaves(x[half:].astype(BF)), "ctx", n, bit)
            yield
            x = x[:half] + order.arrived(got).astype(F32)
            bit //= 2
        result.append(x)
        return
    low = order.leaves(x.astype(BF))
    got = [swap(low[k * rows : (k + 1) * rows], "ctx", n, 2 * k) for k in range(n // 2 - 1, 0, -1)]
    yield
    total = x[:rows]
    for g in order.arrived(*got):
        total = total + g.astype(F32)
    result.append(total)


def sum_steps(x, n, c, bits, order, result):
    for bit in bits:
        half = x.shape[0] // 2
        upper = (c & bit) != 0
        keep = jnp.where(upper, x[half:], x[:half])
        send = jnp.where(upper, x[:half], x[half:])
        got = swap(order.leaves(send), "ctx", n, bit)
        yield
        x = (keep.astype(F32) + order.arrived(got).astype(F32)).astype(BF)
    for bit in bits[:0:-1]:
        upper = (c & bit) != 0
        got = swap(order.leaves(x), "ctx", n, bit)
        yield
        got = order.arrived(got)
        x = jnp.concatenate([jnp.where(upper, got, x), jnp.where(upper, x, got)], axis=0)
    got = swap(order.leaves(x), "ctx", n, bits[0])
    yield
    result += [x, order.arrived(got)]


def short_sum_steps(x, n, c, order, result):
    half = x.shape[0] // 2
    upper = (c & 1) != 0
    keep = jnp.where(upper, x[half:], x[:half])
    send = jnp.where(upper, x[:half], x[half:])
    got = swap(order.leaves(send), "ctx", n, 1)
    yield
    x = keep.astype(F32) + order.arrived(got).astype(F32)
    count = n // 2
    rows = half // count
    z = c >> 1
    low = order.leaves(x.astype(BF))
    total = lax.dynamic_slice_in_dim(x, z * rows, rows, 0)
    got = []
    for j in range(count - 1, 0, -1):
        piece = lax.dynamic_slice_in_dim(low, (z ^ j) * rows, rows, 0)
        got.append(swap(piece, "ctx", n, 2 * j))
    yield
    for g in order.arrived(*got):
        total = total + g.astype(F32)
    mine = order.leaves(total.astype(BF))
    parts = [mine] + [swap(mine, "ctx", n, 2 * j) for j in range(1, count)]
    yield
    parts = order.arrived(*parts)
    x = jnp.zeros((half, x.shape[1]), BF)
    for j, p in enumerate(parts):
        x = lax.dynamic_update_slice_in_dim(x, p, (z ^ j) * rows, 0)
    got = swap(order.leaves(x), "ctx", n, 1)
    yield
    result += [x, order.arrived(got)]


def layer(
    nf,
    nc,
    tokens,
    cotangent,
    block_order,
    query_weight,
    key_weight,
    value_weight,
    out_weight,
    gate_weight,
    up_weight,
    down_weight,
    norm_gains,
    head_gains,
):
    rows, d = tokens.shape
    block_len = rows // 2
    f = lax.axis_index("fsdp")
    c = lax.axis_index("ctx")
    f_arr = f.reshape(1).astype(jnp.int32)
    seq = nc * rows
    tile = min(seq, 1024)
    proj = HEADS * HEAD_DIM
    width = gate_weight.shape[1]
    share = d // nf
    qkv = proj + 2 * HEAD_DIM
    hd = (HEADS, rows, HEAD_DIM)

    wq_far = swap(query_weight, "fsdp", nf, 2)
    tok_all, ahead = gather_ctx(tokens, nc)
    (kvpack,) = call(
        pack_kernel, [((share + 16, 2 * HEAD_DIM), BF)],
        key_weight, value_weight, norm_gains, head_gains,
    )

    slots = jnp.take(block_order.reshape(nc, 2), c ^ jnp.arange(nc), axis=0)
    pos = (slots.reshape(-1, 1) * block_len + jnp.arange(block_len)[None, :]).reshape(seq)
    kpos = pos.reshape(1, seq)
    qpos = pos[:rows].reshape(rows, 1)
    inv_freq = ROPE_BASE ** (-2.0 * jnp.arange(HEAD_DIM // 2, dtype=F32) / HEAD_DIM)
    angles = pos.astype(F32)[:, None] * inv_freq[None, :]
    cos, sin = jnp.cos(angles), jnp.sin(angles)

    wkv = gather_fsdp(kvpack, nf, ahead, cos, sin)
    both = swap(jnp.concatenate([query_weight, follow(wq_far, ahead)], axis=0), "fsdp", nf, 1)
    wq = [query_weight, both[:share], wq_far, both[share:]]
    wo = gather_fsdp(out_weight, nf, both, wkv[1])
    own_ff = (gate_weight, up_weight, down_weight)
    next_ff = [swap(w, "fsdp", nf, 1) for w in lax.optimization_barrier(own_ff + (wo[1],))[:3]]

    big = 16 if seq <= 1024 else 60
    normed, kraw, kv, qraw, q, att, att_low, tot, gains, hg = call(
        functools.partial(front_kernel, nf, tile),
        [
            ((seq, d), BF), ((seq, HEAD_DIM), F32), ((seq, 2 * HEAD_DIM), BF),
            (hd, F32), (hd, BF), (hd, F32), (hd, BF), ((HEADS, rows, 1), F32),
            ((4, d), F32), ((2, HEAD_DIM), F32),
        ],
        f_arr, tok_all, cos, sin, qpos, kpos, *wq, *wkv,
        scratch=[pltpu.VMEM((d, qkv), BF)], smem=1, vmem=big, us=6,
    )
    branch, middle, ff_in = call(
        functools.partial(mid_kernel, nf),
        [((rows, d), F32), ((rows, d), F32), ((rows, d), BF)],
        tokens, gains, att_low, *wo, us=0.6,
    )
    cols = exchange_fsdp(
        [
            jnp.concatenate(
                [att_low[k], lax.dynamic_slice_in_dim(normed[:rows], (f ^ k) * share, share, 1)],
                axis=1,
            )
            for k in range(nf)
        ],
        nf,
    )
    two = 2 * rows
    own, send, pack1, hid, act, slope = call(
        ff_kernel,
        [
            ((rows, d), F32), ((rows, d), BF), ((two, d + width), BF), ((two, width), BF),
            ((2, two, width), F32), ((2, two, width), F32),
        ],
        ff_in, swap(ff_in, "fsdp", nf, 2), *own_ff, *next_ff, us=3.6,
    )
    got1 = swap(pack1, "fsdp", nf, 1)
    output, gml, gain3 = call(
        finish_kernel,
        [((rows, d), BF), ((rows, d), BF), ((1, d), F32)],
        own, swap(send, "fsdp", nf, 2), middle, cotangent, gains, after=cols[1:],
    )
    own, send, pack2, gg = call(
        ff_back_kernel,
        [((rows, d), F32), ((rows, d), BF), ((two, d + 2 * width), BF), ((two, 2 * width), BF)],
        gml, swap(gml, "fsdp", nf, 2), act, slope, *own_ff, *next_ff,
        us=3.6, after=[got1],
    )
    got2 = swap(pack2, "fsdp", nf, 1)
    got = swap(send, "fsdp", nf, 2)
    p_part, up_part = call(
        ff_grad_kernel,
        [((d + width + width // 4, width), BF), ((d, width), BF)],
        pack1, hid, got1, pack2, gg, got2,
        scratch=[
            pltpu.VMEM((2 * two, d), BF),
            pltpu.VMEM((2 * two, width), BF),
            pltpu.VMEM((2 * two, d), BF),
            pltpu.VMEM((2 * two, 2 * width), BF),
        ],
        us=2.5,
    )
    order = Order()
    up_bits = [1 << i for i in range(nc.bit_length() - 1)]
    alt_bits = up_bits[1:2] + up_bits[:1] + up_bits[2:]
    p_sum, q_sum, a_sum, kv_sum = [], [], [], []
    p_steps = sum_steps(p_part, nc, c, alt_bits, order, p_sum)
    next(p_steps)
    gbl, resid, gain12 = call(
        post_kernel,
        [((rows, d), BF), ((rows, d), F32), ((2, d), F32)],
        own, got, middle, branch, cotangent, gains, after=order.last,
    )
    gbl_far = swap(gbl, "fsdp", nf, 2)
    lines = 2 * rows + 16
    wide = 2 * HEAD_DIM
    ybuf, kvw0, kvw1, odd, even = call(
        functools.partial(back_kernel, nf, tile),
        [
            ((lines + 2 * share, wide), BF),
            ((share, wide), F32),
            ((share, wide), F32),
            ((seq // 2, wide), BF),
            ((seq // 2, wide), BF),
        ],
        f_arr, gbl, gain12, gain3, att, tot, q, qraw, kv, normed, kraw, hg, cos, sin, qpos, kpos,
        *wo,
        scratch=[
            pltpu.VMEM((HEADS * rows, HEAD_DIM), BF),
            pltpu.VMEM((HEADS, rows, 1), F32),
            pltpu.VMEM(hd, F32),
            pltpu.VMEM((HEADS * rows, tile), BF),
            pltpu.VMEM((HEADS * rows, tile), BF),
            pltpu.VMEM((d + 8, wide), F32),
            pltpu.VMEM((rows, proj), BF),
        ],
        smem=1, vmem=big, us=9, after=[gbl_far],
    )
    far = swap(order.leaves(ybuf), "fsdp", nf, 2)
    gbl_both = swap(
        order.leaves(jnp.concatenate([gbl, order.arrived(gbl_far)], axis=0)), "fsdp", nf, 1
    )
    next(p_steps)
    gbl_both = order.arrived(gbl_both)
    (q_part,) = call(
        functools.partial(out_grad_kernel, nf),
        [((d + (proj // nf) * 5 // 4, width), BF)],
        up_part, *cols, gbl, gbl_both[:rows], gbl_far, gbl_both[rows:],
        scratch=[pltpu.VMEM((nf * rows, proj // nf), BF), pltpu.VMEM((nf * rows, d), BF)],
        us=1.3,
    )
    q_steps = sum_steps(q_part, nc, c, up_bits, order, q_sum)
    next(q_steps)
    kv_steps = scatter_steps(odd, even, nc, order, kv_sum)
    next(kv_steps)

    far = order.arrived(far)
    cbuf, kvw = call(
        functools.partial(relay_kernel, lines),
        [((2 * lines + share, wide), BF), ((share, wide), F32)],
        ybuf, far, kvw0, kvw1,
    )
    near = swap(order.leaves(cbuf), "fsdp", nf, 1)
    next(p_steps)
    near = order.arrived(near)
    (att_part,) = call(
        functools.partial(query_grad_kernel, lines),
        [((-(-(3 * share + 16) // 128) * 128, wide), BF)],
        ybuf, far, near, kvw, *cols,
        scratch=[pltpu.VMEM((nf * rows, proj), BF), pltpu.VMEM((nf * rows, share), BF)],
    )
    if nc > 8:
        a_steps = sum_steps(att_part, nc, c, up_bits, order, a_sum)
    else:
        a_steps = short_sum_steps(att_part, nc, c, order, a_sum)
    next(a_steps)
    turns = [q_steps, kv_steps, p_steps, a_steps, q_steps, kv_steps, p_steps, a_steps, q_steps]
    turns += [p_steps, a_steps, q_steps, a_steps, q_steps, p_steps]
    for steps in turns:
        next(steps, None)
    for steps in (a_steps, q_steps, p_steps, kv_steps):
        for _ in steps:
            pass

    (input_grad,) = call(
        functools.partial(input_back_kernel, nf),
        [((rows, d), F32)],
        f_arr, tokens, kv_sum[0], ybuf, resid, gains, *wq, *wkv,
        scratch=[pltpu.VMEM((d, qkv), BF)], smem=1, us=1.7,
    )
    upper = (c & up_bits[0]).reshape(1).astype(jnp.int32)
    alt = (c & alt_bits[0]).reshape(1).astype(jnp.int32)
    grad_gate, grad_down = call(
        last_ff_kernel, [((d, width), F32), ((width, d), F32)], alt, *p_sum, smem=1
    )
    grad_up, grad_out = call(
        last_ff_kernel, [((d, width), F32), ((proj // nf, d), F32)],
        upper, *q_sum, smem=1,
    )
    grad_q, grad_k, grad_v, gain0, gain_sum = call(
        last_kernel,
        [
            ((share, proj), F32), ((share, HEAD_DIM), F32), ((share, HEAD_DIM), F32),
            ((share, 1), F32), ((16, wide), F32),
        ],
        upper, *a_sum, query_weight, key_weight, value_weight, smem=1,
    )
    gain0 = gain0.reshape(1, share) / norm_gains[0:1].astype(F32)
    rest = gain_sum[3, : 3 * (d - wide)].reshape(3, d - wide)
    others = jnp.concatenate([gain_sum[:3], rest], axis=1)
    others = lax.dynamic_slice_in_dim(others, f * share, share, 1)
    heads = gain_sum[4].reshape(2, HEAD_DIM)
    return (
        output,
        input_grad,
        grad_q,
        grad_k,
        grad_v,
        grad_out,
        grad_gate,
        grad_up,
        grad_down,
        jnp.concatenate([gain0, others], axis=0),
        lax.dynamic_slice_in_dim(heads, f * (HEAD_DIM // nf), HEAD_DIM // nf, 1),
    )


def solution(mesh):
    row = P(("ctx", "fsdp"), None)
    first, second = P("fsdp", None), P(None, "fsdp")
    body = functools.partial(layer, mesh.shape["fsdp"], mesh.shape["ctx"])
    return jax.shard_map(
        body,
        mesh=mesh,
        in_specs=(row, row, P(), first, first, first, first, second, second, first, second, second),
        out_specs=(row, row, first, first, first, first, second, second, first, second, second),
        check_vma=False,
    )
```

```python
import functools
import math

import jax
import jax.numpy as jnp
from jax import lax
from jax.experimental import pallas as pl
from jax.experimental.pallas import tpu as pltpu
from jax.sharding import PartitionSpec as P

HEADS = 4
HEAD_DIM = 256
NORM_EPS = 1e-06
ROPE_BASE = 1000000.0
BF = jnp.bfloat16
F32 = jnp.float32
MIB = 1024 * 1024


def dot(a, b):
    return lax.dot_general(a, b, (((1,), (0,)), ((), ())), preferred_element_type=F32)


def dot_nt(a, b):
    return lax.dot_general(a, b, (((1,), (1,)), ((), ())), preferred_element_type=F32)


def dot_tn(a, b):
    return lax.dot_general(a, b, (((0,), (0,)), ((), ())), preferred_element_type=F32)


def unit(v):
    r = lax.rsqrt(jnp.mean(v * v, axis=-1, keepdims=True) + NORM_EPS)
    return v * r, r


def norm_back(c, u, r, g):
    cg = c * g
    grad = r * (cg - u * jnp.mean(cg * u, axis=-1, keepdims=True))
    return grad, jnp.sum(c * u, axis=0, keepdims=True)


def rotate(v, cos, sin):
    half = v.shape[-1] // 2
    a, b = v[:, :half], v[:, half:]
    return jnp.concatenate([a * cos - b * sin, b * cos + a * sin], axis=-1)


def rotate_back(v, cos, sin):
    half = v.shape[-1] // 2
    a, b = v[:, :half], v[:, half:]
    return jnp.concatenate([a * cos + b * sin, b * cos - a * sin], axis=-1)


def call(kernel, outs, *args, scratch=(), vmem=16, us=1.0, smem=0, after=()):
    specs = [pl.BlockSpec(memory_space=pltpu.VMEM)] * len(args)
    for i in range(smem):
        specs[i] = pl.BlockSpec(memory_space=pltpu.SMEM)
    specs += [pl.BlockSpec(memory_space=pl.ANY)] * len(after)
    moved = sum(math.prod(a.shape) * a.dtype.itemsize for a in args)
    used, skip = len(args), len(args) + len(after)

    def body(*refs):
        kernel(*refs[:used], *refs[skip:])

    return pl.pallas_call(
        body,
        out_shape=[jax.ShapeDtypeStruct(s, d) for s, d in outs],
        in_specs=specs,
        out_specs=[pl.BlockSpec(memory_space=pltpu.VMEM)] * len(outs),
        scratch_shapes=list(scratch),
        compiler_params=pltpu.CompilerParams(vmem_limit_bytes=vmem * MIB),
        cost_estimate=pl.CostEstimate(
            flops=int(us * 1.1e9), bytes_accessed=moved, transcendentals=0
        ),
    )(*args, *after)


def bound_of(hg):
    peak = jnp.max(jnp.abs(hg[...]), axis=1, keepdims=True)
    return math.sqrt(HEAD_DIM) * peak[0:1, :] * peak[1:2, :]


def tile_loop(count, step):
    if count == 1:
        step(0)
    else:

        def body(t, carry):
            step(t)
            return carry

        lax.fori_loop(0, count, body, 0)


def tile_rows(t, tile, count):
    return pl.ds(pl.multiple_of(t * tile, tile), tile) if count > 1 else slice(None)


def pack_kernel(wk, wv, ng, hg, out):
    share = wk.shape[0]
    out[:share, :HEAD_DIM] = wk[...]
    out[:share, HEAD_DIM:] = wv[...]
    tail = jnp.concatenate(
        [
            ng[...].astype(F32),
            jnp.concatenate(
                [hg[...].astype(F32), jnp.zeros((2, share - hg.shape[1]), F32)], axis=1
            ),
            jnp.zeros((10, share), F32),
        ],
        axis=0,
    )
    out[share:, :] = jnp.zeros((16, out.shape[1]), BF)
    out[share:, :share] = tail.astype(BF)


def ordered(f, parts):
    out = []
    for p in range(len(parts)):
        value = parts[0]
        for k in range(1, len(parts)):
            value = jnp.where(jnp.bitwise_xor(f, k) == p, parts[k], value)
        out.append(value)
    return out


def fill(f, blocks, w, first):
    share = w.shape[0] // len(blocks)
    for k, blk in enumerate(blocks):
        start = pl.multiple_of(jnp.bitwise_xor(f, k) * share, 16)
        w[pl.ds(start, share), first : first + blk.shape[1]] = blk[:share, :]


def front_kernel(nf, tile, f_ref, tok, cos, sin, qpos, kpos, *rest):
    blocks, kv_blocks, rest = rest[:nf], rest[nf : 2 * nf], rest[2 * nf :]
    normed_o, kraw_o, kv_o, qraw_o, q_o, att_o, low_o, tot_o, gains, hg, w = rest
    f = f_ref[0]
    share = w.shape[0] // nf
    rows = qpos.shape[0]
    proj = HEADS * HEAD_DIM
    scale = 1.0 / math.sqrt(HEAD_DIM)
    count = tok.shape[0] // tile
    fill(f, blocks, w, 0)
    fill(f, kv_blocks, w, proj)
    extra = ordered(f, [b[share:, :].astype(F32) for b in kv_blocks])
    gains[...] = jnp.concatenate([e[:4, :share] for e in extra], axis=1)
    hg[...] = jnp.concatenate([e[4:6, : HEAD_DIM // nf] for e in extra], axis=1)
    bound = bound_of(hg)

    def keys(t):
        part = tile_rows(t, tile, count)
        u, _ = unit(tok[part, :].astype(F32))
        normed = (u * gains[0:1, :]).astype(BF)
        normed_o[part, :] = normed
        out = dot(normed, w[:, proj:])
        key = out[:, :HEAD_DIM]
        kraw_o[part, :] = key
        u, _ = unit(key)
        kv_o[part, :HEAD_DIM] = rotate(u * hg[1:2, :], cos[part, :], sin[part, :]).astype(BF)
        kv_o[part, HEAD_DIM:] = out[:, HEAD_DIM:].astype(BF)

    tile_loop(count, keys)
    for h in range(HEADS):
        raw = dot(normed_o[:rows, :], w[:, h * HEAD_DIM : (h + 1) * HEAD_DIM])
        k = jnp.bitwise_xor(f, h)
        qraw_o[k] = raw
        u, _ = unit(raw)
        q_o[k] = rotate(u * hg[0:1, :], cos[:rows, :], sin[:rows, :]).astype(BF)
    for k in range(HEADS):

        def step(t, k=k):
            part = tile_rows(t, tile, count)
            raw = dot_nt(q_o[k], kv_o[part, :HEAD_DIM])
            allowed = kpos[:, part] <= qpos[...]
            terms = jnp.where(allowed, jnp.exp(raw * scale - bound), 0.0)
            total = jnp.sum(terms, axis=1, keepdims=True)
            num = dot(terms.astype(BF), kv_o[part, HEAD_DIM:])
            if count == 1:
                tot_o[k], att_o[k] = total, num
            else:
                tot_o[k] += total
                att_o[k] += num

        if count > 1:
            tot_o[k] = jnp.zeros_like(tot_o[k])
            att_o[k] = jnp.zeros_like(att_o[k])
        tile_loop(count, step)
        att = att_o[k] / tot_o[k]
        att_o[k] = att
        low_o[k] = att.astype(BF)


def mid_kernel(nf, tok, gains, att, *rest):
    wo = rest[:nf]
    branch_o, middle_o, ff_o = rest[nf:]
    branch = None
    for k in range(nf):
        term = dot(att[k], wo[k][...])
        branch = term if branch is None else branch + term
    branch_o[...] = branch
    u, _ = unit(branch)
    middle = tok[...].astype(F32) + u * gains[1:2, :]
    middle_o[...] = middle
    u, _ = unit(middle)
    ff_o[...] = (u * gains[2:3, :]).astype(BF)


def gelu_parts(v):
    t = jnp.tanh(0.7978845608028654 * (v + 0.044715 * v * v * v))
    half = 0.5 * (1.0 + t)
    slope = half + 0.5 * v * (1.0 - t * t) * 0.7978845608028654 * (1.0 + 3 * 0.044715 * v * v)
    return v * half, slope


def ff_kernel(mine, other, wg0, wu0, wd0, wg1, wu1, wd1, own_o, send_o, pack_o, hid_o, a_o, b_o):
    rows, d = mine.shape
    pack_o[:rows, :d] = mine[...]
    pack_o[rows:, :d] = other[...]
    x = pack_o[:, :d]
    mixed = None
    for i, (wg, wu, wd) in enumerate(((wg0, wu0, wd0), (wg1, wu1, wd1))):
        gate = dot(x, wg[...])
        up = dot(x, wu[...])
        value, slope = gelu_parts(gate)
        a_o[i] = value.astype(BF)
        b_o[i] = (up * slope).astype(BF)
        hidden = (value * up).astype(BF)
        if i == 0:
            hid_o[...] = hidden
        else:
            pack_o[:, d:] = hidden
        term = dot(hidden, wd[...])
        mixed = term if mixed is None else mixed + term
    own_o[...] = mixed[:rows, :]
    send_o[...] = mixed[rows:, :].astype(BF)


def finish_kernel(own, got, middle, cot, gains, out_o, low_o, gain_o):
    u, r = unit(own[...] + got[...].astype(F32))
    out_o[...] = (middle[...] + u * gains[3:4, :]).astype(BF)
    grad, gain = norm_back(cot[...].astype(F32), u, r, gains[3:4, :])
    low_o[...] = grad.astype(BF)
    gain_o[...] = gain


def ff_back_kernel(
    mine, other, a, b, wg0, wu0, wd0, wg1, wu1, wd1, own_o, send_o, pack_o, gg_o
):
    rows, d = mine.shape
    width = wg0.shape[1]
    pack_o[:rows, :d] = mine[...]
    pack_o[rows:, :d] = other[...]
    c = pack_o[:, :d]
    total = None
    for i, (wg, wu, wd) in enumerate(((wg0, wu0, wd0), (wg1, wu1, wd1))):
        gh = dot_nt(c, wd[...])
        gg = (gh * b[i].astype(F32)).astype(BF)
        gu = (gh * a[i].astype(F32)).astype(BF)
        if i == 0:
            gg_o[:, :width] = gg
            gg_o[:, width:] = gu
        else:
            pack_o[:, d : d + width] = gg
            pack_o[:, d + width :] = gu
        term = dot_nt(gg, wg[...]) + dot_nt(gu, wu[...])
        total = term if total is None else total + term
    own_o[...] = total[:rows, :]
    send_o[...] = total[rows:, :].astype(BF)


def fold(out, at, grad, wide):
    rows = grad.shape[0]
    out[at : at + rows, :] = grad[:, :wide].astype(BF)
    strip = rows // 4
    parts = [grad[i * strip : (i + 1) * strip, wide:] for i in range(4)]
    out[at + rows : at + rows + strip, :] = jnp.concatenate(parts, axis=1).astype(BF)


def unfold(full, at, out):
    rows, wide = out.shape[0], full.shape[1]
    out[:, :wide] = full[at : at + rows]
    strip, piece = rows // 4, wide // 4
    for i in range(4):
        out[i * strip : (i + 1) * strip, wide:] = full[
            at + rows : at + rows + strip, i * piece : (i + 1) * piece
        ]


def ff_grad_kernel(pack1, hid, got1, pack2, gg, got2, gate_o, up_o, x_s, h_s, c_s, g_s):
    rows, width = hid.shape
    d = x_s.shape[1]
    x_s[:rows, :] = pack1[:, :d]
    x_s[rows:, :] = got1[:, :d]
    h_s[:rows, :] = hid[...]
    h_s[rows:, :] = got1[:, d:]
    c_s[:rows, :] = pack2[:, :d]
    c_s[rows:, :] = got2[:, :d]
    g_s[:rows, :] = gg[...]
    g_s[rows:, :] = got2[:, d:]
    gate_o[:d, :] = dot_tn(x_s[...], g_s[:, :width]).astype(BF)
    up_o[...] = dot_tn(x_s[...], g_s[:, width:]).astype(BF)
    fold(gate_o, d, dot_tn(h_s[...], c_s[...]), width)


def post_kernel(own, got, middle, branch, cot, gains, gbl_o, resid_o, gain_o):
    um, rm = unit(middle[...])
    grad, gain2 = norm_back(own[...] + got[...].astype(F32), um, rm, gains[2:3, :])
    grad_middle = cot[...].astype(F32) + grad
    resid_o[...] = grad_middle
    ub, rb = unit(branch[...])
    grad_branch, gain1 = norm_back(grad_middle, ub, rb, gains[1:2, :])
    gbl_o[...] = grad_branch.astype(BF)
    gain_o[...] = jnp.concatenate([gain1, gain2], axis=0)


def back_kernel(
    nf, tile, f_ref, gbl, gain12, gain3, att, tot, q, qraw, kv, normed, kraw, hg, cos, sin, qpos,
    kpos, *rest,
):
    wo = rest[:nf]
    far_o, own_o, next_o, odd_o, even_o, sg_s, tg_s, acc, s_s, e_s, kvw_s, gq_s = rest[nf:]
    f = f_ref[0]
    scale = 1.0 / math.sqrt(HEAD_DIM)
    rows, d = gbl.shape
    bound = bound_of(hg)
    count = kv.shape[0] // tile
    for k in range(HEADS):
        ga = dot_nt(gbl[...], wo[k][...])
        inv = 1.0 / tot[k]
        sg_s[k * rows : (k + 1) * rows, :] = (ga * inv).astype(BF)
        tg_s[k] = -jnp.sum(ga * att[k], axis=1, keepdims=True) * inv

    def step(t):
        part = tile_rows(t, tile, count)
        allowed = kpos[:, part] <= qpos[...]
        for k in range(HEADS):
            mine = slice(k * rows, (k + 1) * rows)
            raw = dot_nt(q[k], kv[part, :HEAD_DIM])
            terms = jnp.where(allowed, jnp.exp(raw * scale - bound), 0.0)
            e_s[mine, :] = terms.astype(BF)
            gp = dot_nt(sg_s[mine, :], kv[part, HEAD_DIM:])
            s = (terms * (gp + tg_s[k]) * scale).astype(BF)
            s_s[mine, :] = s
            term = dot(s, kv[part, :HEAD_DIM])
            if count == 1:
                acc[k] = term
            else:
                acc[k] += term
        queries = q[...].reshape(HEADS * rows, HEAD_DIM)
        c = rotate_back(dot_tn(s_s[...], queries), cos[part, :], sin[part, :])
        u, r = unit(kraw[part, :])
        gk, gain = norm_back(c, u, r, hg[1:2, :])
        gkl = gk.astype(BF)
        gvl = dot_tn(e_s[...], sg_s[...]).astype(BF)
        kk = dot_tn(normed[part, :], gkl)
        vv = dot_tn(normed[part, :], gvl)
        if count == 1:
            kvw_s[:d, :HEAD_DIM] = kk
            kvw_s[:d, HEAD_DIM:] = vv
            kvw_s[d : d + 1, :HEAD_DIM] = gain
        else:
            kvw_s[:d, :HEAD_DIM] += kk
            kvw_s[:d, HEAD_DIM:] += vv
            kvw_s[d : d + 1, :HEAD_DIM] += gain
        for j in range(tile // rows):
            out = even_o if j % 2 == 0 else odd_o
            start = (j // 2) * rows
            if count > 1:
                start = pl.multiple_of(t * (tile // 2) + start, rows)
            out[pl.ds(start, rows), :HEAD_DIM] = gkl[j * rows : (j + 1) * rows, :]
            out[pl.ds(start, rows), HEAD_DIM:] = gvl[j * rows : (j + 1) * rows, :]

    if count > 1:
        acc[...] = jnp.zeros_like(acc)
        kvw_s[...] = jnp.zeros_like(kvw_s)
    tile_loop(count, step)
    share = own_o.shape[0]
    lines = 2 * rows + 16
    for k, out in enumerate((own_o, next_o, None, None)):
        start = pl.multiple_of(jnp.bitwise_xor(f, k) * share, 16)
        chunk = kvw_s[pl.ds(start, share), :]
        if out is not None:
            out[...] = chunk
        else:
            at = lines + (k - 2) * share
            far_o[at : at + share, :] = chunk.astype(BF)
    gain = None
    for k in range(HEADS):
        u, r = unit(qraw[k])
        c = rotate_back(acc[k], cos[:rows, :], sin[:rows, :])
        grad, g = norm_back(c, u, r, hg[0:1, :])
        gain = g if gain is None else gain + g
        h = jnp.bitwise_xor(f, k)
        gq_s[:, pl.ds(pl.multiple_of(h * HEAD_DIM, HEAD_DIM), HEAD_DIM)] = grad.astype(BF)
    wide = 2 * HEAD_DIM
    far_o[:rows, :] = gq_s[:, :wide]
    far_o[rows : 2 * rows, :] = gq_s[:, wide:]
    three = jnp.concatenate([gain12[...], gain3[...]], axis=0)
    tail = jnp.concatenate(
        [three[i : i + 1, wide:] for i in range(3)] + [jnp.zeros((1, 4 * wide - 3 * d), F32)],
        axis=1,
    )
    heads = jnp.concatenate([gain, kvw_s[d : d + 1, :HEAD_DIM]], axis=1)
    pad = jnp.zeros((11, wide), F32)
    far_o[2 * rows : lines, :] = jnp.concatenate(
        [three[:, :wide], tail, heads, pad], axis=0
    ).astype(BF)


def relay_kernel(lines, mine, far, own, nxt, out_o, own_o):
    share = own.shape[0]
    out_o[:lines, :] = mine[:lines, :]
    out_o[lines : 2 * lines, :] = far[:lines, :]
    out_o[2 * lines :, :] = (nxt[...] + far[lines + share :, :].astype(F32)).astype(BF)
    own_o[...] = own[...] + far[lines : lines + share, :].astype(F32)


def query_grad_kernel(lines, mine, far, got, own, *rest):
    cols, (out_o, g_s, n_s) = rest[:4], rest[4:]
    rows, share = cols[0].shape[0], n_s.shape[1]
    wide = mine.shape[1]
    gain = None
    for k, (ref, at) in enumerate(((mine, 0), (got, 0), (far, 0), (got, lines))):
        mine_rows = slice(k * rows, (k + 1) * rows)
        g_s[mine_rows, :wide] = ref[at : at + rows, :]
        g_s[mine_rows, wide:] = ref[at + rows : at + 2 * rows, :]
        n_s[mine_rows, :] = cols[k][:, cols[k].shape[1] - share :]
        part = ref[at + 2 * rows : at + lines, :].astype(F32)
        gain = part if gain is None else gain + part
    qw = dot_tn(n_s[...], g_s[...])
    out_o[:share, :] = qw[:, :wide].astype(BF)
    out_o[share : 2 * share, :] = qw[:, wide:].astype(BF)
    out_o[2 * share : 3 * share, :] = (own[...] + got[2 * lines :, :].astype(F32)).astype(BF)
    out_o[3 * share : 3 * share + 16, :] = gain.astype(BF)
    out_o[3 * share + 16 :, :] = jnp.zeros((out_o.shape[0] - 3 * share - 16, wide), BF)


def out_grad_kernel(nf, up, *refs):
    cols, gbl, (out_o, a_s, b_s) = refs[:nf], refs[nf : 2 * nf], refs[2 * nf :]
    rows = gbl[0].shape[0]
    for k in range(nf):
        a_s[k * rows : (k + 1) * rows, :] = cols[k][:, : a_s.shape[1]]
        b_s[k * rows : (k + 1) * rows, :] = gbl[k][...]
    out_o[: up.shape[0], :] = up[...]
    fold(out_o, up.shape[0], dot_tn(a_s[...], b_s[...]), up.shape[1])


def joined(upper, mine, got):
    a, b = mine[...].astype(F32), got[...].astype(F32)
    return jnp.concatenate([jnp.where(upper, b, a), jnp.where(upper, a, b)], axis=0)


def last_ff_kernel(upper_ref, mine, got, first_o, second_o):
    full = joined(upper_ref[0] != 0, mine, got)
    rows = first_o.shape[0]
    first_o[...] = full[:rows]
    unfold(full, rows, second_o)


def last_kernel(upper_ref, mine, got, wq, wk, wv, q_o, k_o, v_o, p_o, rest_o):
    share = wq.shape[0]
    full = joined(upper_ref[0] != 0, mine, got)
    wide = full.shape[1]
    q_o[:, :wide] = full[:share]
    q_o[:, wide:] = full[share : 2 * share]
    k_o[...] = full[2 * share : 3 * share, :HEAD_DIM]
    v_o[...] = full[2 * share : 3 * share, HEAD_DIM:]
    total = jnp.sum(q_o[...] * wq[...].astype(F32), axis=1, keepdims=True)
    total += jnp.sum(k_o[...] * wk[...].astype(F32), axis=1, keepdims=True)
    p_o[...] = total + jnp.sum(v_o[...] * wv[...].astype(F32), axis=1, keepdims=True)
    rest_o[...] = full[3 * share : 3 * share + 16]


def input_back_kernel(nf, f_ref, tok, gkv, gq, resid, gains, *rest):
    blocks, kv_blocks, (grad_o, w) = rest[:nf], rest[nf : 2 * nf], rest[2 * nf :]
    rows = tok.shape[0]
    proj = HEADS * HEAD_DIM
    fill(f_ref[0], blocks, w, 0)
    fill(f_ref[0], kv_blocks, w, proj)
    low = gkv[...].astype(BF)
    wide = 2 * HEAD_DIM
    gn = dot_nt(gq[:rows, :], w[:, :wide]) + dot_nt(gq[rows : 2 * rows, :], w[:, wide:proj])
    gn = gn + dot_nt(low, w[:, proj:])
    u, r = unit(tok[...].astype(F32))
    gx, _ = norm_back(gn, u, r, gains[0:1, :])
    grad_o[...] = resid[...] + gx


def swap(x, axis, n, bit):
    return lax.ppermute(x, axis, [(i, i ^ bit) for i in range(n)])


class Order:
    def __init__(self):
        self.last = ()

    def arrived(self, *xs):
        out = lax.optimization_barrier(tuple(xs) + self.last)[: len(xs)]
        return out if len(xs) > 1 else out[0]

    def leaves(self, x):
        self.last = (x,)
        return x


def follow(x, *earlier):
    return lax.optimization_barrier((x,) + earlier)[0]


def gather_fsdp(x, n, *earlier):
    far = swap(x, "fsdp", n, 2)
    both = swap(jnp.concatenate([x, follow(far, *earlier)], axis=0), "fsdp", n, 1)
    rows = x.shape[0]
    return [x, both[:rows], far, both[rows:]]


def exchange_fsdp(blocks, n):
    return [b if k == 0 else swap(b, "fsdp", n, k) for k, b in enumerate(blocks)]


def gather_ctx(x, n):
    if n > 8:
        bit = 1
        while bit < n:
            x = jnp.concatenate([x, swap(x, "ctx", n, bit)], axis=0)
            bit *= 2
        return x, x
    far = {k: swap(x, "ctx", n, k) for k in range(n - 2, 0, -2)}
    rows = x.shape[0]
    first = swap(jnp.concatenate([x, far[2]], axis=0), "ctx", n, 1)
    ahead = jnp.concatenate([far[k] for k in range(4, n, 2)], axis=0)
    second = swap(ahead, "ctx", n, 1)
    parts = [x, first[:rows], far[2], first[rows:]]
    for i, k in enumerate(range(4, n, 2)):
        parts += [far[k], second[i * rows : (i + 1) * rows]]
    return jnp.concatenate(parts, axis=0), ahead


def scatter_steps(odd, even, n, order, result):
    got = swap(order.leaves(odd), "ctx", n, 1)
    yield
    x = even.astype(F32) + order.arrived(got).astype(F32)
    rows = x.shape[0] * 2 // n
    if n > 8:
        bit = n // 2
        while bit > 1:
            half = x.shape[0] // 2
            got = swap(order.leaves(x[half:].astype(BF)), "ctx", n, bit)
            yield
            x = x[:half] + order.arrived(got).astype(F32)
            bit //= 2
        result.append(x)
        return
    low = order.leaves(x.astype(BF))
    got = [swap(low[k * rows : (k + 1) * rows], "ctx", n, 2 * k) for k in range(n // 2 - 1, 0, -1)]
    yield
    total = x[:rows]
    for g in order.arrived(*got):
        total = total + g.astype(F32)
    result.append(total)


def sum_steps(x, n, c, bits, order, result):
    for bit in bits:
        half = x.shape[0] // 2
        upper = (c & bit) != 0
        keep = jnp.where(upper, x[half:], x[:half])
        send = jnp.where(upper, x[:half], x[half:])
        got = swap(order.leaves(send), "ctx", n, bit)
        yield
        x = (keep.astype(F32) + order.arrived(got).astype(F32)).astype(BF)
    for bit in bits[:0:-1]:
        upper = (c & bit) != 0
        got = swap(order.leaves(x), "ctx", n, bit)
        yield
        got = order.arrived(got)
        x = jnp.concatenate([jnp.where(upper, got, x), jnp.where(upper, x, got)], axis=0)
    got = swap(order.leaves(x), "ctx", n, bits[0])
    yield
    result += [x, order.arrived(got)]


def short_sum_steps(x, n, c, order, result):
    half = x.shape[0] // 2
    upper = (c & 1) != 0
    keep = jnp.where(upper, x[half:], x[:half])
    send = jnp.where(upper, x[:half], x[half:])
    got = swap(order.leaves(send), "ctx", n, 1)
    yield
    x = keep.astype(F32) + order.arrived(got).astype(F32)
    count = n // 2
    rows = half // count
    z = c >> 1
    low = order.leaves(x.astype(BF))
    total = lax.dynamic_slice_in_dim(x, z * rows, rows, 0)
    got = []
    for j in range(count - 1, 0, -1):
        piece = lax.dynamic_slice_in_dim(low, (z ^ j) * rows, rows, 0)
        got.append(swap(piece, "ctx", n, 2 * j))
    yield
    for g in order.arrived(*got):
        total = total + g.astype(F32)
    mine = order.leaves(total.astype(BF))
    parts = [mine] + [swap(mine, "ctx", n, 2 * j) for j in range(1, count)]
    yield
    parts = order.arrived(*parts)
    x = jnp.zeros((half, x.shape[1]), BF)
    for j, p in enumerate(parts):
        x = lax.dynamic_update_slice_in_dim(x, p, (z ^ j) * rows, 0)
    got = swap(order.leaves(x), "ctx", n, 1)
    yield
    result += [x, order.arrived(got)]


def layer(
    nf,
    nc,
    tokens,
    cotangent,
    block_order,
    query_weight,
    key_weight,
    value_weight,
    out_weight,
    gate_weight,
    up_weight,
    down_weight,
    norm_gains,
    head_gains,
):
    rows, d = tokens.shape
    block_len = rows // 2
    f = lax.axis_index("fsdp")
    c = lax.axis_index("ctx")
    f_arr = f.reshape(1).astype(jnp.int32)
    seq = nc * rows
    tile = min(seq, 1024)
    proj = HEADS * HEAD_DIM
    width = gate_weight.shape[1]
    share = d // nf
    qkv = proj + 2 * HEAD_DIM
    hd = (HEADS, rows, HEAD_DIM)

    wq_far = swap(query_weight, "fsdp", nf, 2)
    tok_all, ahead = gather_ctx(tokens, nc)
    (kvpack,) = call(
        pack_kernel, [((share + 16, 2 * HEAD_DIM), BF)],
        key_weight, value_weight, norm_gains, head_gains,
    )

    slots = jnp.take(block_order.reshape(nc, 2), c ^ jnp.arange(nc), axis=0)
    pos = (slots.reshape(-1, 1) * block_len + jnp.arange(block_len)[None, :]).reshape(seq)
    kpos = pos.reshape(1, seq)
    qpos = pos[:rows].reshape(rows, 1)
    inv_freq = ROPE_BASE ** (-2.0 * jnp.arange(HEAD_DIM // 2, dtype=F32) / HEAD_DIM)
    angles = pos.astype(F32)[:, None] * inv_freq[None, :]
    cos, sin = jnp.cos(angles), jnp.sin(angles)

    wkv = gather_fsdp(kvpack, nf, ahead, cos, sin)
    both = swap(jnp.concatenate([query_weight, follow(wq_far, ahead)], axis=0), "fsdp", nf, 1)
    wq = [query_weight, both[:share], wq_far, both[share:]]
    wo = gather_fsdp(out_weight, nf, both, wkv[1])
    own_ff = (gate_weight, up_weight, down_weight)
    next_ff = [swap(w, "fsdp", nf, 1) for w in lax.optimization_barrier(own_ff + (wo[1],))[:3]]

    big = 16 if seq <= 1024 else 60
    normed, kraw, kv, qraw, q, att, att_low, tot, gains, hg = call(
        functools.partial(front_kernel, nf, tile),
        [
            ((seq, d), BF), ((seq, HEAD_DIM), F32), ((seq, 2 * HEAD_DIM), BF),
            (hd, F32), (hd, BF), (hd, F32), (hd, BF), ((HEADS, rows, 1), F32),
            ((4, d), F32), ((2, HEAD_DIM), F32),
        ],
        f_arr, tok_all, cos, sin, qpos, kpos, *wq, *wkv,
        scratch=[pltpu.VMEM((d, qkv), BF)], smem=1, vmem=big, us=6,
    )
    branch, middle, ff_in = call(
        functools.partial(mid_kernel, nf),
        [((rows, d), F32), ((rows, d), F32), ((rows, d), BF)],
        tokens, gains, att_low, *wo, us=0.6,
    )
    cols = exchange_fsdp(
        [
            jnp.concatenate(
                [att_low[k], lax.dynamic_slice_in_dim(normed[:rows], (f ^ k) * share, share, 1)],
                axis=1,
            )
            for k in range(nf)
        ],
        nf,
    )
    two = 2 * rows
    own, send, pack1, hid, act, slope = call(
        ff_kernel,
        [
            ((rows, d), F32), ((rows, d), BF), ((two, d + width), BF), ((two, width), BF),
            ((2, two, width), BF), ((2, two, width), BF),
        ],
        ff_in, swap(ff_in, "fsdp", nf, 2), *own_ff, *next_ff, us=3.6,
    )
    got1 = swap(pack1, "fsdp", nf, 1)
    output, gml, gain3 = call(
        finish_kernel,
        [((rows, d), BF), ((rows, d), BF), ((1, d), F32)],
        own, swap(send, "fsdp", nf, 2), middle, cotangent, gains, after=cols[1:],
    )
    own, send, pack2, gg = call(
        ff_back_kernel,
        [((rows, d), F32), ((rows, d), BF), ((two, d + 2 * width), BF), ((two, 2 * width), BF)],
        gml, swap(gml, "fsdp", nf, 2), act, slope, *own_ff, *next_ff,
        us=3.6, after=[got1],
    )
    got2 = swap(pack2, "fsdp", nf, 1)
    got = swap(send, "fsdp", nf, 2)
    p_part, up_part = call(
        ff_grad_kernel,
        [((d + width + width // 4, width), BF), ((d, width), BF)],
        pack1, hid, got1, pack2, gg, got2,
        scratch=[
            pltpu.VMEM((2 * two, d), BF),
            pltpu.VMEM((2 * two, width), BF),
            pltpu.VMEM((2 * two, d), BF),
            pltpu.VMEM((2 * two, 2 * width), BF),
        ],
        us=2.5,
    )
    order = Order()
    up_bits = [1 << i for i in range(nc.bit_length() - 1)]
    alt_bits = up_bits[1:2] + up_bits[:1] + up_bits[2:]
    p_sum, q_sum, a_sum, kv_sum = [], [], [], []
    p_steps = sum_steps(p_part, nc, c, alt_bits, order, p_sum)
    next(p_steps)
    gbl, resid, gain12 = call(
        post_kernel,
        [((rows, d), BF), ((rows, d), F32), ((2, d), F32)],
        own, got, middle, branch, cotangent, gains, after=order.last,
    )
    gbl_far = swap(gbl, "fsdp", nf, 2)
    lines = 2 * rows + 16
    wide = 2 * HEAD_DIM
    ybuf, kvw0, kvw1, odd, even = call(
        functools.partial(back_kernel, nf, tile),
        [
            ((lines + 2 * share, wide), BF),
            ((share, wide), F32),
            ((share, wide), F32),
            ((seq // 2, wide), BF),
            ((seq // 2, wide), BF),
        ],
        f_arr, gbl, gain12, gain3, att, tot, q, qraw, kv, normed, kraw, hg, cos, sin, qpos, kpos,
        *wo,
        scratch=[
            pltpu.VMEM((HEADS * rows, HEAD_DIM), BF),
            pltpu.VMEM((HEADS, rows, 1), F32),
            pltpu.VMEM(hd, F32),
            pltpu.VMEM((HEADS * rows, tile), BF),
            pltpu.VMEM((HEADS * rows, tile), BF),
            pltpu.VMEM((d + 8, wide), F32),
            pltpu.VMEM((rows, proj), BF),
        ],
        smem=1, vmem=big, us=9, after=[gbl_far],
    )
    far = swap(order.leaves(ybuf), "fsdp", nf, 2)
    gbl_both = swap(
        order.leaves(jnp.concatenate([gbl, order.arrived(gbl_far)], axis=0)), "fsdp", nf, 1
    )
    next(p_steps)
    gbl_both = order.arrived(gbl_both)
    (q_part,) = call(
        functools.partial(out_grad_kernel, nf),
        [((d + (proj // nf) * 5 // 4, width), BF)],
        up_part, *cols, gbl, gbl_both[:rows], gbl_far, gbl_both[rows:],
        scratch=[pltpu.VMEM((nf * rows, proj // nf), BF), pltpu.VMEM((nf * rows, d), BF)],
        us=1.3,
    )
    q_steps = sum_steps(q_part, nc, c, up_bits, order, q_sum)
    next(q_steps)
    kv_steps = scatter_steps(odd, even, nc, order, kv_sum)
    next(kv_steps)

    far = order.arrived(far)
    cbuf, kvw = call(
        functools.partial(relay_kernel, lines),
        [((2 * lines + share, wide), BF), ((share, wide), F32)],
        ybuf, far, kvw0, kvw1,
    )
    near = swap(order.leaves(cbuf), "fsdp", nf, 1)
    next(p_steps)
    near = order.arrived(near)
    (att_part,) = call(
        functools.partial(query_grad_kernel, lines),
        [((-(-(3 * share + 16) // 128) * 128, wide), BF)],
        ybuf, far, near, kvw, *cols,
        scratch=[pltpu.VMEM((nf * rows, proj), BF), pltpu.VMEM((nf * rows, share), BF)],
    )
    if nc > 8:
        a_steps = sum_steps(att_part, nc, c, up_bits, order, a_sum)
    else:
        a_steps = short_sum_steps(att_part, nc, c, order, a_sum)
    next(a_steps)
    turns = [q_steps, kv_steps, p_steps, a_steps, q_steps, kv_steps, p_steps, a_steps, q_steps]
    turns += [p_steps, a_steps, q_steps, a_steps, q_steps, p_steps]
    for steps in turns:
        next(steps, None)
    for steps in (a_steps, q_steps, p_steps, kv_steps):
        for _ in steps:
            pass

    (input_grad,) = call(
        functools.partial(input_back_kernel, nf),
        [((rows, d), F32)],
        f_arr, tokens, kv_sum[0], ybuf, resid, gains, *wq, *wkv,
        scratch=[pltpu.VMEM((d, qkv), BF)], smem=1, us=1.7,
    )
    upper = (c & up_bits[0]).reshape(1).astype(jnp.int32)
    alt = (c & alt_bits[0]).reshape(1).astype(jnp.int32)
    grad_gate, grad_down = call(
        last_ff_kernel, [((d, width), F32), ((width, d), F32)], alt, *p_sum, smem=1
    )
    grad_up, grad_out = call(
        last_ff_kernel, [((d, width), F32), ((proj // nf, d), F32)],
        upper, *q_sum, smem=1,
    )
    grad_q, grad_k, grad_v, gain0, gain_sum = call(
        last_kernel,
        [
            ((share, proj), F32), ((share, HEAD_DIM), F32), ((share, HEAD_DIM), F32),
            ((share, 1), F32), ((16, wide), F32),
        ],
        upper, *a_sum, query_weight, key_weight, value_weight, smem=1,
    )
    gain0 = gain0.reshape(1, share) / norm_gains[0:1].astype(F32)
    rest = gain_sum[3, : 3 * (d - wide)].reshape(3, d - wide)
    others = jnp.concatenate([gain_sum[:3], rest], axis=1)
    others = lax.dynamic_slice_in_dim(others, f * share, share, 1)
    heads = gain_sum[4].reshape(2, HEAD_DIM)
    return (
        output,
        input_grad,
        grad_q,
        grad_k,
        grad_v,
        grad_out,
        grad_gate,
        grad_up,
        grad_down,
        jnp.concatenate([gain0, others], axis=0),
        lax.dynamic_slice_in_dim(heads, f * (HEAD_DIM // nf), HEAD_DIM // nf, 1),
    )


def solution(mesh):
    row = P(("ctx", "fsdp"), None)
    first, second = P("fsdp", None), P(None, "fsdp")
    body = functools.partial(layer, mesh.shape["fsdp"], mesh.shape["ctx"])
    return jax.shard_map(
        body,
        mesh=mesh,
        in_specs=(row, row, P(), first, first, first, first, second, second, first, second, second),
        out_specs=(row, row, first, first, first, first, second, second, first, second, second),
        check_vma=False,
    )
```
